32 devices in a mesh: slab: 4 (over y, x), brick: 8 (over z, core).
Axes of the slice: x: 2, y: 2, z: 4, core: 2. Of those that a mesh axis runs over, the one named last changes fastest.
Arguments:
- embed: bfloat16 [32768, 512], P(('slab', 'brick')), may hold values from -6 to 6
- cotangent: bfloat16 [32768, 512], P(('slab', 'brick')), may hold values from -6 to 6
- basis: bfloat16 [16, 16, 32768], P(None, None, ('slab', 'brick')), may hold values from -4 to 4
- triplet_row_index: int32 [16, 32768], P(None, ('slab', 'brick')), may hold values from 0 to 1535
- triplet_slot_count: int32 [32768], P(('slab', 'brick')), may hold values from 1 to 16, as said below
- outgoing_edge_rows: int32 [4, 4096], P(None, ('slab', 'brick')), may hold values from 0 to 1023
- residual_weight: bfloat16 [512, 512], replicated, may hold values from -0.25 to 0.25
- down_weight: bfloat16 [512, 64], replicated, may hold values from -0.25 to 0.25
- up_weight: bfloat16 [64, 512], replicated, may hold values from -0.75 to 0.75
- basis_weight: bfloat16 [16, 64], replicated, may hold values from -1.5 to 1.5
Outputs:
- edge_embedding_gradient: bfloat16 [32768, 512], P(('slab', 'brick'))
- residual_weight_gradient: float32 [512, 512], replicated
- down_weight_gradient: float32 [512, 64], replicated
- up_weight_gradient: float32 [64, 512], replicated
- basis_weight_gradient: float32 [16, 64], replicated
The draws below stay inside these ranges and needn't reach their ends.
Inputs may be any that keep to these rules, and one draw needn't show every extreme that they name: `triplet_row_index`: indices refer to the extended table of the edge's own brick. `triplet_slot_count`: slots at or past the count are empty; in every brick some edge fills all 16 slots; bricks differ in density. `outgoing_edge_rows`: local row numbers within the sending brick; a row may appear more than once.
All inputs are finite; a program needn't handle non-finite values.
Results may differ from the reference program's by a relative error of at most 0.006.
Values may be sent and summed in bfloat16 or wider, within the bound.
No kernel may reach another device: no remote copies, remote signals or barrier semaphores. Data moves between devices by JAX's collectives and lax.ppermute only.
A program may use at most 64 MiB of HBM per device.

```python
import jax
import jax.numpy as jnp
from jax import lax

D = 512
TRIPLET_WIDTH = 64
BASIS_FUNCTIONS = 16
TRIP = 16
E_DEV = 1024
GHOST = 128
EDGES = 32768
GHOSTS = 4096
N_SLAB = 4
N_BRICK = 8


def draw_triplet_slot_count(key, part):
    devices = EDGES // E_DEV
    ceiling = jax.random.randint(jax.random.fold_in(key, 11), (devices, 1), TRIP // 4, TRIP + 1)
    raw = jax.random.randint(jax.random.fold_in(key, 12), (devices, E_DEV), 0, 1048576)
    counts = 1 + raw % ceiling
    first = lax.broadcasted_iota(jnp.int32, (devices, E_DEV), 1) == 0
    return jnp.where(first, TRIP, counts).reshape(EDGES).astype(jnp.int32)


def place_ends(entries, own_key, low, largest):
    longest = entries.shape.index(max(entries.shape))
    spots = []
    for shift in (0, 1):
        where = [jax.random.randint(jax.random.fold_in(own_key, axis), (), 0, length) for axis, length in enumerate(entries.shape)]
        where[longest] = (where[longest] + shift) % entries.shape[longest]
        spots.append(tuple(where))
    return entries.at[spots[0]].set(low).at[spots[1]].set(largest)


def level_of(own_key, extent, pieces, least, top_value):
    def one(position, blocks):
        heights = jax.random.uniform(jax.random.fold_in(jax.random.fold_in(own_key, 6), position), (blocks,), jnp.float32, least / len(pieces), top_value / len(pieces))
        return jnp.repeat(jnp.exp(heights), extent[position] // blocks).reshape((-1,) + (1,) * (len(extent) - position - 1))

    gain = one(*pieces[0])
    for cut in pieces[1:]:
        gain = gain * one(*cut)
    return gain


def bell_draw(stream_key, dims, width, bound, cuts=(), kind=jnp.bfloat16):
    gain = level_of(stream_key, dims, cuts, -0.22, 0.18) if cuts else 1.0
    drawn = jax.random.normal(stream_key, dims, jnp.float32) * width * gain
    return jnp.minimum(jnp.maximum(drawn, -bound), bound).astype(kind)


def setup_inputs(seed: int = 0) -> dict:
    streams_of = jax.random.split(jax.random.key(seed), 11)
    return {
        "embed": bell_draw(streams_of[0], (EDGES, D), 1.0, 6.0, ((0, 32),)),
        "cotangent": bell_draw(streams_of[1], (EDGES, D), 1.0, 6.0, ((0, 32),)),
        "basis": bell_draw(streams_of[2], (TRIP, BASIS_FUNCTIONS, EDGES), 1.0, 4.0, ((2, 32),)),
        "triplet_row_index": place_ends(jax.random.randint(streams_of[3], (TRIP, EDGES), 0, E_DEV + 4 * GHOST), jax.random.fold_in(streams_of[3], 1), 0, (E_DEV + 4 * GHOST) - 1).astype(jnp.int32),
        "triplet_slot_count": draw_triplet_slot_count(jax.random.fold_in(streams_of[10], 71), 0),
        "outgoing_edge_rows": place_ends(jax.random.randint(streams_of[5], (4, GHOSTS), 0, E_DEV), jax.random.fold_in(streams_of[5], 1), 0, E_DEV - 1).astype(jnp.int32),
        "residual_weight": bell_draw(streams_of[6], (D, D), D ** -0.5, 0.25),
        "down_weight": bell_draw(streams_of[7], (D, TRIPLET_WIDTH), D ** -0.5, 0.25),
        "up_weight": bell_draw(streams_of[8], (TRIPLET_WIDTH, D), TRIPLET_WIDTH ** -0.5, 0.75),
        "basis_weight": bell_draw(streams_of[9], (BASIS_FUNCTIONS, TRIPLET_WIDTH), BASIS_FUNCTIONS ** -0.5, 1.5),
    }


def silu_grad(value):
    sig = jax.nn.sigmoid(value)
    return sig * (1.0 + value * (1.0 - sig))

def pick_cols(edge_table_rows, rows):
    return edge_table_rows[:, rows]

def add_cols(target, rows, values):
    return target.at[:, rows].add(values)

def reference(embed, cotangent, basis, triplet_row_index, triplet_slot_count, outgoing_edge_rows, residual_weight, down_weight, up_weight, basis_weight):
    slabs = N_SLAB
    bricks = N_BRICK
    count_dev = slabs * bricks
    pre = lax.dot_general(down_weight, embed, (((0,), (1,)), ((), ())), preferred_element_type=jnp.float32)
    proj = jax.nn.silu(pre).astype(jnp.bfloat16)
    proj_dev = proj.reshape(TRIPLET_WIDTH, slabs, bricks, E_DEV).transpose(1, 2, 0, 3)
    send = outgoing_edge_rows.reshape(4, slabs, bricks, GHOST)
    picker = jax.vmap(jax.vmap(pick_cols))
    blocks = [jnp.roll(picker(proj_dev, send[0]), 1, 0), jnp.roll(picker(proj_dev, send[1]), -1, 0), jnp.roll(picker(proj_dev, send[2]), 1, 1), jnp.roll(picker(proj_dev, send[3]), -1, 1)]
    edge_table_rows = jnp.concatenate([proj_dev] + blocks, axis=3).reshape(count_dev, TRIPLET_WIDTH, E_DEV + 4 * GHOST)
    basis_on_shard = basis.reshape(TRIP, BASIS_FUNCTIONS, count_dev, E_DEV).transpose(2, 0, 1, 3)
    slot_index_shard = triplet_row_index.reshape(TRIP, count_dev, E_DEV).transpose(1, 0, 2)
    slot_count_total = triplet_slot_count.reshape(count_dev, E_DEV)
    upstream_gradient_shard = cotangent.reshape(count_dev, E_DEV, D)
    basis_weight_float = basis_weight.astype(jnp.float32)

    def triplet_partial(inputs):
        table_d, basis_shard, index_d, count_d, cot_d = inputs
        weight_list = jnp.einsum('unz,nh->huz', basis_shard.astype(jnp.float32), basis_weight_float)
        live = (jnp.arange(TRIP)[:, None] < count_d[None, :]).astype(jnp.float32)
        gathered = table_d[:, index_d].astype(jnp.float32)
        tsum = lax.optimization_barrier(jnp.sum(weight_list * gathered * live[None], axis=1))
        activation_value = jax.nn.silu(tsum).astype(jnp.bfloat16)
        dsum = lax.dot_general(up_weight, cot_d, (((1,), (1,)), ((), ())), preferred_element_type=jnp.float32)
        dt = dsum * silu_grad(tsum)
        weight_gradient_list = (dt[:, None, :] * gathered * live[None]).astype(jnp.bfloat16)
        partial_basis_gradient = jnp.einsum('yqi,wyi->qw', basis_shard.astype(jnp.float32), weight_gradient_list.astype(jnp.float32))
        dhx = dt[:, None, :] * weight_list * live[None]
        table_gradient = jnp.zeros(table_d.shape, jnp.float32).at[:, index_d].add(dhx)
        return (table_gradient, activation_value, partial_basis_gradient)
    table_gradient, activation_value, partial_basis_gradient = lax.map(triplet_partial, (edge_table_rows, basis_on_shard, slot_index_shard, slot_count_total, upstream_gradient_shard))
    basis_weight_gradient = lax.optimization_barrier(jnp.sum(partial_basis_gradient, axis=0))
    table_gradient = table_gradient.reshape(slabs, bricks, TRIPLET_WIDTH, E_DEV + 4 * GHOST)
    dproj = table_gradient[..., :E_DEV]
    adder = jax.vmap(jax.vmap(add_cols))
    shifts = [(1, 0), (-1, 0), (1, 1), (-1, 1)]
    for step in range(4):
        by, mesh_dimension = shifts[step]
        back = table_gradient[..., E_DEV + step * GHOST:E_DEV + (step + 1) * GHOST]
        back = jnp.roll(back, -by, mesh_dimension)
        dproj = adder(dproj, send[step], back)
    dproj = dproj.transpose(2, 0, 1, 3).reshape(TRIPLET_WIDTH, EDGES)
    act_all = activation_value.transpose(1, 0, 2).reshape(TRIPLET_WIDTH, EDGES)
    up_weight_gradient = lax.dot_general(act_all, cotangent, (((1,), (0,)), ((), ())), preferred_element_type=jnp.float32)
    dpre = (dproj * silu_grad(pre)).astype(jnp.bfloat16)
    down_weight_gradient = lax.dot_general(embed, dpre, (((0,), (1,)), ((), ())), preferred_element_type=jnp.float32)
    down_term = lax.dot_general(dpre, down_weight, (((0,), (1,)), ((), ())), preferred_element_type=jnp.float32)
    res_pre = jnp.dot(embed, residual_weight, preferred_element_type=jnp.float32)
    dres = (cotangent.astype(jnp.float32) * silu_grad(res_pre)).astype(jnp.bfloat16)
    residual_weight_gradient = lax.dot_general(embed, dres, (((0,), (0,)), ((), ())), preferred_element_type=jnp.float32)
    res_term = lax.dot_general(dres, residual_weight, (((1,), (1,)), ((), ())), preferred_element_type=jnp.float32)
    edge_embedding_gradient = (res_term + down_term).astype(jnp.bfloat16)
    return (edge_embedding_gradient, residual_weight_gradient, down_weight_gradient, up_weight_gradient, basis_weight_gradient)
```

```python
import functools

import jax
import jax.numpy as jnp
from jax import lax
from jax.experimental import pallas as pl
from jax.experimental.pallas import tpu as pltpu
from jax.sharding import PartitionSpec as P

AXES = ("slab", "brick")
LANES = 256
F32 = jnp.float32
BF16 = jnp.bfloat16


def dot(a, b, dims, precision=None):
    return lax.dot_general(a, b, (dims, ((), ())), precision=precision, preferred_element_type=F32)


NN = ((1,), (0,))
NT = ((1,), (1,))
TN = ((0,), (0,))


def sigmoid(value):
    return 1.0 / (1.0 + jnp.exp(-value))


def silu_grad(value):
    sig = sigmoid(value)
    return sig * (1.0 + value * (1.0 - sig))


def onehot(low):
    rows = lax.broadcasted_iota(jnp.int32, (LANES, low.shape[1]), 0)
    return jnp.where(rows == low, 1.0, 0.0).astype(BF16)


def stacked(table):
    return jnp.concatenate(
        [table[:, g * LANES : (g + 1) * LANES] for g in range(table.shape[1] // LANES)], axis=0
    )


def unstacked(blocks, width):
    return jnp.concatenate(
        [blocks[g * width : (g + 1) * width] for g in range(blocks.shape[0] // width)], axis=1
    )


def chosen(blocks, high, width):
    total = jnp.zeros((width, blocks.shape[1]), F32)
    for g in range(blocks.shape[0] // width):
        total = jnp.where(high == g, blocks[g * width : (g + 1) * width], total)
    return total


def spread(values, high, groups):
    zero = jnp.zeros_like(values)
    return jnp.concatenate([jnp.where(high == g, values, zero) for g in range(groups)], axis=0)


def project_kernel(embed_ref, down_ref, rows_ref, pre_ref, proj_ref, *send_refs):
    pre = dot(down_ref[...], embed_ref[...], NT)
    pre_ref[...] = pre
    proj = (pre * sigmoid(pre)).astype(BF16)
    proj_ref[...] = proj
    table = stacked(proj)
    width = proj.shape[0]
    for k, send_ref in enumerate(send_refs):
        index = rows_ref[k : k + 1, :]
        picked = dot(table, onehot(index & (LANES - 1)), NN)
        send_ref[...] = chosen(picked, index // LANES, width).astype(BF16)


def project(embed, down_t, outgoing):
    rows, width = embed.shape[0], down_t.shape[0]
    ghost = outgoing.shape[1]
    return pl.pallas_call(
        project_kernel,
        out_shape=[
            jax.ShapeDtypeStruct((width, rows), F32),
            jax.ShapeDtypeStruct((width, rows), BF16),
        ]
        + [jax.ShapeDtypeStruct((width, ghost), BF16)] * 4,
        compiler_params=pltpu.CompilerParams(vmem_limit_bytes=16 * 2**20),
        name="project",
    )(embed, down_t, outgoing)


def triplet_kernel(
    proj_ref,
    g0_ref,
    g1_ref,
    g2_ref,
    g3_ref,
    basis_ref,
    index_ref,
    count_ref,
    up_ref,
    cotangent_ref,
    bw_ref,
    own_ref,
    ghost_ref,
    grads_ref,
    table_ref,
    weight_ref,
    hot_ref,
    picked_ref,
    dw_ref,
    tsum_ref,
    dt_ref,
    acc_ref,
):
    width, rows = proj_ref.shape
    trips = index_ref.shape[0]
    nbasis = bw_ref.shape[0]
    own_groups = rows // LANES
    ghosts = jnp.concatenate([g0_ref[...], g1_ref[...], g2_ref[...], g3_ref[...]], axis=1)
    table_ref[: own_groups * width, :] = stacked(proj_ref[...])
    table_ref[own_groups * width :, :] = stacked(ghosts)
    groups = table_ref.shape[0] // width
    tiles = rows // LANES

    span = trips * nbasis
    fold = jnp.where(
        lax.broadcasted_iota(jnp.int32, (nbasis, span), 1) % nbasis
        == lax.broadcasted_iota(jnp.int32, (nbasis, span), 0),
        1.0,
        0.0,
    )
    wide = dot(bw_ref[...], fold.astype(BF16), TN).astype(BF16)
    own_slot = lax.broadcasted_iota(jnp.int32, (trips, width, span), 0) == (
        lax.broadcasted_iota(jnp.int32, (trips, width, span), 2) // nbasis
    )
    diagonal = jnp.where(own_slot, wide[None], jnp.zeros((), BF16)).reshape(trips * width, span)
    weight_ref[...] = dot(diagonal, basis_ref[...], NN)

    tsum_ref[...] = jnp.zeros_like(tsum_ref)

    def lookup(j, t):
        at = pl.ds(t * LANES, LANES)
        index = index_ref[pl.ds(j, 1), at]
        high = jnp.where(j < count_ref[:, at], index // LANES, -1)
        return at, index & (LANES - 1), high

    def forward(j, carry):
        for t in range(tiles):
            at, low, high = lookup(j, t)
            hot = onehot(low)
            hot_ref[j, :, at] = hot
            picked = chosen(dot(table_ref[...], hot, NN), high, width)
            picked_ref[j, :, at] = picked.astype(BF16)
            tsum_ref[:, at] += weight_ref[pl.ds(j * width, width), at] * picked
        return carry

    lax.fori_loop(0, trips, forward, 0)

    tsum = tsum_ref[...]
    sig = sigmoid(tsum)
    act = (tsum * sig).astype(BF16)
    cotangent = cotangent_ref[...]
    inner = cotangent.shape[1]
    grads_ref[:, :inner] = dot(act, cotangent, NN).astype(BF16)
    dsum = dot(up_ref[...], cotangent, NT)
    dt_ref[...] = dsum * (sig * (1.0 + tsum * (1.0 - sig)))
    acc_ref[...] = jnp.zeros_like(acc_ref)

    def backward(j, carry):
        parts = []
        for t in range(tiles):
            at, low, high = lookup(j, t)
            dt = dt_ref[:, at]
            dw_ref[pl.ds(j * width, width), at] = (dt * picked_ref[j, :, at].astype(F32)).astype(BF16)
            terms = (dt * weight_ref[pl.ds(j * width, width), at]).astype(BF16)
            parts.append(spread(terms, high, groups))
        acc_ref[...] += dot(jnp.concatenate(parts, axis=1), hot_ref[j], NT)
        return carry

    lax.fori_loop(0, trips, backward, 0)

    own_ref[...] = unstacked(acc_ref[: own_groups * width, :], width)
    ghost_ref[...] = unstacked(acc_ref[own_groups * width :, :], width).astype(BF16)
    full = dot(dw_ref[...], basis_ref[...], NT).reshape(trips, width, span)
    kept = jnp.sum(jnp.where(own_slot, full, 0.0), axis=0)
    folded = dot(kept, fold, NT, lax.Precision.HIGHEST)
    pad = grads_ref.shape[1] - inner - nbasis
    grads_ref[:, inner:] = jnp.concatenate(
        [folded, jnp.zeros((width, pad), F32)], axis=1
    ).astype(BF16)


def triplets(proj, ghosts, basis, index, count, up_weight, cotangent, basis_weight):
    width, rows = proj.shape
    trips, nbasis = basis.shape[:2]
    ghost = ghosts[0].shape[1]
    inner = cotangent.shape[1]
    table_rows = rows + 4 * ghost
    groups = table_rows // LANES
    return pl.pallas_call(
        triplet_kernel,
        out_shape=[
            jax.ShapeDtypeStruct((width, rows), F32),
            jax.ShapeDtypeStruct((width, 4 * ghost), BF16),
            jax.ShapeDtypeStruct((width, inner + 128), BF16),
        ],
        scratch_shapes=[
            pltpu.VMEM((groups * width, LANES), BF16),
            pltpu.VMEM((trips * width, rows), F32),
            pltpu.VMEM((trips, LANES, rows), BF16),
            pltpu.VMEM((trips, width, rows), BF16),
            pltpu.VMEM((trips * width, rows), BF16),
            pltpu.VMEM((width, rows), F32),
            pltpu.VMEM((width, rows), F32),
            pltpu.VMEM((groups * width, LANES), F32),
        ],
        compiler_params=pltpu.CompilerParams(vmem_limit_bytes=40 * 2**20),
        name="triplets",
    )(
        proj,
        *ghosts,
        basis.reshape(trips * nbasis, rows),
        index,
        count.reshape(1, rows),
        up_weight,
        cotangent,
        basis_weight,
    )


def collect_kernel(
    own_ref, b0_ref, b1_ref, b2_ref, b3_ref, rows_ref, pre_ref, embed_ref, dpre_ref, grad_ref
):
    width, rows = own_ref.shape
    groups = rows // LANES
    acc = jnp.zeros((groups * width, LANES), F32)
    for k, back_ref in enumerate((b0_ref, b1_ref, b2_ref, b3_ref)):
        index = rows_ref[k : k + 1, :]
        acc += dot(spread(back_ref[...], index // LANES, groups), onehot(index & (LANES - 1)), NT)
    dproj = own_ref[...] + unstacked(acc, width)
    dpre = (dproj * silu_grad(pre_ref[...])).astype(BF16)
    dpre_ref[...] = dpre
    grad_ref[...] = dot(dpre, embed_ref[...], NN).astype(BF16)


def collect(own, backs, outgoing, pre, embed):
    return pl.pallas_call(
        collect_kernel,
        out_shape=[
            jax.ShapeDtypeStruct(own.shape, BF16),
            jax.ShapeDtypeStruct((own.shape[0], embed.shape[1]), BF16),
        ],
        compiler_params=pltpu.CompilerParams(vmem_limit_bytes=16 * 2**20),
        name="collect",
    )(own, *backs, outgoing, pre, embed)


def passed_along(value, axis, steps):
    count = lax.axis_size(axis)
    return lax.ppermute(value, axis, [(i, (i + steps) % count) for i in range(count)])


def swapped(value, axis, bit):
    return lax.ppermute(value, axis, [(i, i ^ bit) for i in range(lax.axis_size(axis))])


def bits_of(axis):
    bit, bits = 1, []
    while bit < lax.axis_size(axis):
        bits.append((axis, bit))
        bit *= 2
    return bits


def side(step):
    axis, bit = step
    return (lax.axis_index(axis) // bit) % 2


def halved(value, step):
    rows = value.shape[0] // 2
    upper = side(step)
    mine = lax.dynamic_slice_in_dim(value, upper * rows, rows, 0)
    other = lax.dynamic_slice_in_dim(value, (1 - upper) * rows, rows, 0)
    return mine + swapped(other, *step)


def doubled(value, step):
    other = swapped(value, *step)
    upper = side(step)
    return jnp.where(
        upper == 1,
        jnp.concatenate([other, value], axis=0),
        jnp.concatenate([value, other], axis=0),
    )


def shards(
    embed,
    cotangent,
    basis,
    triplet_row_index,
    triplet_slot_count,
    outgoing_edge_rows,
    residual_weight,
    down_weight,
    up_weight,
    basis_weight,
):
    inner = embed.shape[1]
    ghost = outgoing_edge_rows.shape[1]
    nbasis = basis.shape[1]
    down_t = down_weight.T
    moves = (("slab", 1), ("slab", -1), ("brick", 1), ("brick", -1))

    pre, proj, *sends = project(embed, down_t, outgoing_edge_rows)
    ghosts = [passed_along(sends[k], *moves[k]) for k in range(4)]

    res_pre = jnp.dot(embed, residual_weight, preferred_element_type=F32)
    dres = (cotangent.astype(F32) * silu_grad(res_pre)).astype(BF16)
    residual_grad = dot(embed, dres, TN).astype(BF16)

    scattered = [("brick", 1)] + bits_of("slab")
    summed = bits_of("brick")[1:]
    for step in scattered:
        residual_grad = halved(residual_grad, step)

    own, ghost_terms, grads = triplets(
        proj, ghosts, basis, triplet_row_index, triplet_slot_count, up_weight, cotangent, basis_weight
    )
    backs = [
        passed_along(ghost_terms[:, k * ghost : (k + 1) * ghost], moves[k][0], -moves[k][1])
        for k in range(4)
    ]
    dpre, down_grad = collect(own, backs, outgoing_edge_rows, pre, embed)

    rest = jnp.concatenate([down_grad, grads], axis=1)
    for step in summed[::-1]:
        residual_grad = residual_grad + swapped(residual_grad, *step)
        rest = rest + swapped(rest, *step)
    for step in scattered[::-1]:
        residual_grad = doubled(residual_grad, step)
        rest = rest + swapped(rest, *step)

    res_term = dot(dres, residual_weight, NT)
    down_term = dot(dpre, down_weight, ((0,), (1,)))
    edge_grad = (res_term + down_term).astype(BF16)
    rest = rest.astype(F32)
    return (
        edge_grad,
        residual_grad.astype(F32),
        rest[:, :inner].T,
        rest[:, inner : 2 * inner],
        rest[:, 2 * inner : 2 * inner + nbasis].T,
    )


def solution(mesh):
    both = P(AXES, None)
    in_specs = (both, both, P(None, None, AXES), P(None, AXES), P(AXES), P(None, AXES)) + (P(),) * 4
    out_specs = (both, P(), P(), P(), P())
    return jax.shard_map(shards, mesh=mesh, in_specs=in_specs, out_specs=out_specs, check_vma=False)
```

```python
import jax
import jax.numpy as jnp
from jax import lax
from jax.experimental import pallas as pl
from jax.experimental.pallas import tpu as pltpu
from jax.sharding import PartitionSpec as P

AXES = ("slab", "brick")
LANES = 256
F32 = jnp.float32
BF16 = jnp.bfloat16
NN = ((1,), (0,))
NT = ((1,), (1,))
TN = ((0,), (0,))
VMEM = pl.BlockSpec(memory_space=pltpu.VMEM)
HBM = pl.BlockSpec(memory_space=pltpu.HBM)


def dot(a, b, dims, precision=None):
    return lax.dot_general(a, b, (dims, ((), ())), precision=precision, preferred_element_type=F32)


def like(*arrays):
    return [jax.ShapeDtypeStruct(a.shape, a.dtype) for a in arrays]


def limits(mib):
    return pltpu.CompilerParams(vmem_limit_bytes=mib * 2**20)


def sigmoid(value):
    return 1.0 / (1.0 + jnp.exp(-value))


def silu_grad(value):
    sig = sigmoid(value)
    return sig * (1.0 + value * (1.0 - sig))


def parity(axis):
    return lax.axis_index(axis) % 2 == 1


def onehot(low):
    rows = lax.broadcasted_iota(jnp.int32, (LANES, low.shape[1]), 0).astype(jnp.int16)
    return jnp.where(rows == low.astype(jnp.int16), jnp.ones((), BF16), jnp.zeros((), BF16))


def stacked(table):
    return jnp.concatenate(
        [table[:, g * LANES : (g + 1) * LANES] for g in range(table.shape[1] // LANES)], axis=0
    )


def unstacked(blocks, width):
    return jnp.concatenate(
        [blocks[g * width : (g + 1) * width] for g in range(blocks.shape[0] // width)], axis=1
    )


def chosen(blocks, high, width):
    total = jnp.zeros((width, blocks.shape[1]), F32)
    for g in range(blocks.shape[0] // width):
        total = jnp.where(high == g, blocks[g * width : (g + 1) * width], total)
    return total


def spread(values, high, groups):
    zero = jnp.zeros_like(values)
    return jnp.concatenate([jnp.where(high == g, values, zero) for g in range(groups)], axis=0)


def pair_lists(rows_ref):
    lists = []
    for first, axis in ((0, "slab"), (2, "brick")):
        odd = parity(axis)
        up, down = rows_ref[first : first + 1, :], rows_ref[first + 1 : first + 2, :]
        lists += [jnp.where(odd, down, up), jnp.where(odd, up, down)]
    return lists


def paired(value, axis, first):
    count = lax.axis_size(axis)
    pairs = []
    for i in range(first, count, 2):
        j = (i + 1) % count
        pairs += [(i, j), (j, i)]
    return lax.ppermute(value, axis, pairs)


def pair_exchange(values):
    spots = (("slab", 0), ("slab", 1), ("brick", 0), ("brick", 1))
    sent = {k: paired(values[k], *spots[k]) for k in (3, 1, 0, 2)}
    return [sent[k] for k in range(4)]


def project_kernel(
    embed_ref, down_ref, rows_ref, pre_ref, proj_ref, s0, s1, s2, s3, embed_v, down_v, rows_v, sems
):
    copies = [
        pltpu.make_async_copy(source, target, sems.at[i])
        for i, (source, target) in enumerate(
            ((embed_ref, embed_v), (down_ref, down_v), (rows_ref, rows_v))
        )
    ]
    for copy in copies:
        copy.start()
    for copy in copies:
        copy.wait()
    pre = dot(down_v[...], embed_v[...], NT)
    pre_ref[...] = pre
    proj = (pre * sigmoid(pre)).astype(BF16)
    proj_ref[...] = proj
    table = stacked(proj)
    for index, send_ref in zip(pair_lists(rows_v), (s0, s1, s2, s3)):
        picked = dot(table, onehot(index & (LANES - 1)), NN)
        send_ref[...] = chosen(picked, index // LANES, proj.shape[0]).astype(BF16)


def project(embed, down_t, outgoing):
    rows, width = embed.shape[0], down_t.shape[0]
    ghost = jax.ShapeDtypeStruct((width, outgoing.shape[1]), BF16)
    return pl.pallas_call(
        project_kernel,
        in_specs=[HBM] * 3,
        out_specs=[VMEM] * 9,
        out_shape=[
            jax.ShapeDtypeStruct((width, rows), F32),
            jax.ShapeDtypeStruct((width, rows), BF16),
        ]
        + [ghost] * 4
        + like(embed, down_t, outgoing),
        scratch_shapes=[pltpu.SemaphoreType.DMA((3,))],
        compiler_params=limits(12),
        name="project",
    )(embed, down_t, outgoing)


def residual_kernel(embed_ref, weight_ref, *refs):
    count = (len(refs) - 5) // 2
    sources, targets = refs[:count], refs[count : 2 * count]
    dres_ref, mine_ref, other_ref, grad_ref, sems = refs[2 * count :]
    copies = [
        pltpu.make_async_copy(source, target, sems.at[i])
        for i, (source, target) in enumerate(zip(sources, targets))
    ]
    for copy in copies:
        copy.start()
    copies[0].wait()
    cotangent_v = targets[0]
    rows = embed_ref.shape[0]
    block = min(rows, LANES)
    for start in range(0, rows, block):
        at = pl.ds(start, block)
        res_pre = dot(embed_ref[at, :], weight_ref[...], NN)
        dres_ref[at, :] = (cotangent_v[at, :].astype(F32) * silu_grad(res_pre)).astype(BF16)
    grad_ref[...] = dot(embed_ref[...], dres_ref[...], TN).astype(BF16)
    half = grad_ref.shape[0] // 2
    upper = lax.axis_index("brick") % 2
    mine_ref[...] = grad_ref[pl.ds(upper * half, half), :]
    other_ref[...] = grad_ref[pl.ds((1 - upper) * half, half), :]
    for copy in copies[1:]:
        copy.wait()


def residual(embed, weight, *staged):
    inner = weight.shape[0]
    half = jax.ShapeDtypeStruct((inner // 2, weight.shape[1]), BF16)
    out_shape = like(*staged) + like(embed) + [half] * 2
    return pl.pallas_call(
        residual_kernel,
        in_specs=[VMEM] * 2 + [HBM] * len(staged),
        out_specs=[VMEM] * len(out_shape),
        out_shape=out_shape,
        scratch_shapes=[pltpu.VMEM(weight.shape, BF16), pltpu.SemaphoreType.DMA((len(staged),))],
        compiler_params=limits(16),
        name="residual",
    )(embed, weight, *staged)


def triplet_kernel(
    proj_ref,
    g0_ref,
    g1_ref,
    g2_ref,
    g3_ref,
    basis_ref,
    index_ref,
    count_ref,
    up_ref,
    cotangent_ref,
    bw_ref,
    own_ref,
    t0_ref,
    t1_ref,
    t2_ref,
    t3_ref,
    grads_ref,
    table_ref,
    weight_ref,
    hot_ref,
    picked_ref,
    dw_ref,
    tsum_ref,
    dt_ref,
    acc_ref,
):
    width, rows = proj_ref.shape
    trips = index_ref.shape[0]
    nbasis = bw_ref.shape[0]
    own_groups = rows // LANES
    blocks = []
    for a_ref, b_ref, axis in ((g0_ref, g1_ref, "slab"), (g2_ref, g3_ref, "brick")):
        odd = parity(axis)
        a, b = a_ref[...], b_ref[...]
        blocks += [jnp.where(odd, a, b), jnp.where(odd, b, a)]
    table_ref[: own_groups * width, :] = stacked(proj_ref[...])
    table_ref[own_groups * width :, :] = stacked(jnp.concatenate(blocks, axis=1))
    groups = table_ref.shape[0] // width
    tiles = rows // LANES

    span = trips * nbasis
    fold = jnp.where(
        lax.broadcasted_iota(jnp.int32, (nbasis, span), 1) % nbasis
        == lax.broadcasted_iota(jnp.int32, (nbasis, span), 0),
        1.0,
        0.0,
    )
    wide = dot(bw_ref[...], fold.astype(BF16), TN).astype(BF16)
    own_slot = lax.broadcasted_iota(jnp.int32, (trips, width, span), 0) == (
        lax.broadcasted_iota(jnp.int32, (trips, width, span), 2) // nbasis
    )
    diagonal = jnp.where(own_slot, wide[None], jnp.zeros((), BF16)).reshape(trips * width, span)
    weight_ref[...] = dot(diagonal, basis_ref[...], NN)

    tsum_ref[...] = jnp.zeros_like(tsum_ref)

    def lookup(j, t):
        at = pl.ds(t * LANES, LANES)
        index = index_ref[pl.ds(j, 1), at]
        high = jnp.where(j < count_ref[:, at], index // LANES, -1)
        return at, index & (LANES - 1), high

    def forward(j, carry):
        for t in range(tiles):
            at, low, high = lookup(j, t)
            hot = onehot(low)
            hot_ref[j, :, at] = hot
            picked = chosen(dot(table_ref[...], hot, NN), high, width)
            picked_ref[j, :, at] = picked.astype(BF16)
            tsum_ref[:, at] += weight_ref[pl.ds(j * width, width), at] * picked
        return carry

    lax.fori_loop(0, trips, forward, 0, unroll=8)

    tsum = tsum_ref[...]
    sig = sigmoid(tsum)
    act = (tsum * sig).astype(BF16)
    cotangent = cotangent_ref[...]
    inner = cotangent.shape[1]
    grads_ref[:, :inner] = dot(act, cotangent, NN).astype(BF16)
    dsum = dot(up_ref[...], cotangent, NT)
    dt_ref[...] = dsum * (sig * (1.0 + tsum * (1.0 - sig)))
    acc_ref[...] = jnp.zeros_like(acc_ref)

    def backward(j, carry):
        parts = []
        for t in range(tiles):
            at, low, high = lookup(j, t)
            dt = dt_ref[:, at]
            dw_ref[pl.ds(j * width, width), at] = (dt * picked_ref[j, :, at].astype(F32)).astype(BF16)
            terms = (dt * weight_ref[pl.ds(j * width, width), at]).astype(BF16)
            parts.append(spread(terms, high, groups))
        acc_ref[...] += dot(jnp.concatenate(parts, axis=1), hot_ref[j], NT)
        return carry

    lax.fori_loop(0, trips, backward, 0, unroll=8)

    own_ref[...] = unstacked(acc_ref[: own_groups * width, :], width)
    ghost_terms = unstacked(acc_ref[own_groups * width :, :], width).astype(BF16)
    ghost = t0_ref.shape[1]
    for first, axis, a_ref, b_ref in ((0, "slab", t0_ref, t1_ref), (2, "brick", t2_ref, t3_ref)):
        odd = parity(axis)
        prev = ghost_terms[:, first * ghost : (first + 1) * ghost]
        following = ghost_terms[:, (first + 1) * ghost : (first + 2) * ghost]
        a_ref[...] = jnp.where(odd, prev, following)
        b_ref[...] = jnp.where(odd, following, prev)
    full = dot(dw_ref[...], basis_ref[...], NT).reshape(trips, width, span)
    kept = jnp.sum(jnp.where(own_slot, full, 0.0), axis=0)
    folded = dot(kept, fold, NT, lax.Precision.HIGHEST)
    pad = grads_ref.shape[1] - inner - nbasis
    grads_ref[:, inner:] = jnp.concatenate(
        [folded, jnp.zeros((width, pad), F32)], axis=1
    ).astype(BF16)


def triplets(proj, ghosts, basis, index, count, up_weight, cotangent, basis_weight):
    width, rows = proj.shape
    trips = index.shape[0]
    ghost = ghosts[0].shape[1]
    inner = cotangent.shape[1]
    groups = (rows + 4 * ghost) // LANES
    operands = (proj, *ghosts, basis, index, count, up_weight, cotangent, basis_weight)
    out_shape = (
        [jax.ShapeDtypeStruct((width, rows), F32)]
        + like(*ghosts)
        + [jax.ShapeDtypeStruct((width, inner + 128), BF16)]
    )
    return pl.pallas_call(
        triplet_kernel,
        in_specs=[VMEM] * len(operands),
        out_specs=[VMEM] * len(out_shape),
        out_shape=out_shape,
        scratch_shapes=[
            pltpu.VMEM((groups * width, LANES), BF16),
            pltpu.VMEM((trips * width, rows), F32),
            pltpu.VMEM((trips, LANES, rows), BF16),
            pltpu.VMEM((trips, width, rows), BF16),
            pltpu.VMEM((trips * width, rows), BF16),
            pltpu.VMEM((width, rows), F32),
            pltpu.VMEM((width, rows), F32),
            pltpu.VMEM((groups * width, LANES), F32),
        ],
        compiler_params=limits(28),
        name="triplets",
    )(*operands)


def collect_kernel(
    own_ref,
    b0_ref,
    b1_ref,
    b2_ref,
    b3_ref,
    rows_ref,
    pre_ref,
    embed_ref,
    grads_ref,
    dpre_ref,
    mine_ref,
    other_ref,
    all_ref,
):
    width, rows = own_ref.shape
    groups = rows // LANES
    acc = jnp.zeros((groups * width, LANES), F32)
    for index, back_ref in zip(pair_lists(rows_ref), (b0_ref, b1_ref, b2_ref, b3_ref)):
        acc += dot(spread(back_ref[...], index // LANES, groups), onehot(index & (LANES - 1)), NT)
    dproj = own_ref[...] + unstacked(acc, width)
    dpre = (dproj * silu_grad(pre_ref[...])).astype(BF16)
    dpre_ref[...] = dpre
    inner = embed_ref.shape[1]
    all_ref[:, :inner] = dot(dpre, embed_ref[...], NN).astype(BF16)
    all_ref[:, inner:] = grads_ref[...]
    half = width // 2
    upper = lax.axis_index("brick") % 2
    mine_ref[...] = all_ref[pl.ds(upper * half, half), :]
    other_ref[...] = all_ref[pl.ds((1 - upper) * half, half), :]


def collect(own, backs, outgoing, pre, embed, grads):
    width = own.shape[0]
    total = embed.shape[1] + grads.shape[1]
    half = jax.ShapeDtypeStruct((width // 2, total), BF16)
    operands = (own, *backs, outgoing, pre, embed, grads)
    return pl.pallas_call(
        collect_kernel,
        in_specs=[VMEM] * len(operands),
        out_specs=[VMEM] * 3,
        out_shape=[jax.ShapeDtypeStruct(own.shape, BF16), half, half],
        scratch_shapes=[pltpu.VMEM((width, total), BF16)],
        compiler_params=limits(12),
        name="collect",
    )(*operands)


def edge_kernel(dres_ref, weight_ref, dpre_ref, down_ref, out_ref):
    rows = dres_ref.shape[0]
    block = min(rows, LANES)
    for start in range(0, rows, block):
        at = pl.ds(start, block)
        res_term = dot(dres_ref[at, :], weight_ref[...], NT)
        out_ref[at, :] = (res_term + dot(dpre_ref[:, at], down_ref[...], TN)).astype(BF16)


def edge_gradient(dres, weight, dpre, down_t):
    rows, inner = dres.shape
    return pl.pallas_call(
        edge_kernel,
        in_specs=[VMEM] * 4,
        out_specs=VMEM,
        out_shape=jax.ShapeDtypeStruct((rows, inner), BF16),
        compiler_params=limits(12),
        cost_estimate=pl.CostEstimate(
            flops=2 * rows * inner * (inner + down_t.shape[0]),
            bytes_accessed=4 * rows * inner,
            transcendentals=0,
        ),
        name="edge_gradient",
    )(dres, weight, dpre, down_t)


def finish_kernel(offsets, *refs):
    count = len(offsets)
    kept, sent = refs[:count], refs[count : 2 * count]
    mine_ref, other_ref, residual_ref, down_ref, up_ref, basis_ref, all_ref = refs[2 * count :]
    upper = lax.axis_index("brick") % 2
    slab = lax.axis_index("slab")
    step = kept[0].shape[0]
    half = residual_ref.shape[0] // 2
    for offset, kept_ref, sent_ref in zip(offsets, kept, sent):
        place = (slab ^ offset) * step
        residual_ref[pl.ds(upper * half + place, step), :] = kept_ref[...].astype(F32)
        residual_ref[pl.ds((1 - upper) * half + place, step), :] = sent_ref[...].astype(F32)
    rows, inner = mine_ref.shape[0], down_ref.shape[1]
    all_ref[pl.ds(upper * rows, rows), :] = mine_ref[...].astype(F32)
    all_ref[pl.ds((1 - upper) * rows, rows), :] = other_ref[...].astype(F32)
    down_ref[...] = all_ref[:, :inner]
    up_ref[...] = all_ref[:, inner : 2 * inner]
    basis_ref[...] = all_ref[:, 2 * inner :].T[: basis_ref.shape[0], :]


def finish(kept, sent, mine, other, inner, nbasis):
    offsets = sorted(kept)
    width = 2 * mine.shape[0]
    operands = [kept[o] for o in offsets] + [sent[o] for o in offsets] + [mine, other]
    return pl.pallas_call(
        lambda *refs: finish_kernel(offsets, *refs),
        in_specs=[VMEM] * len(operands),
        out_specs=[VMEM] * 4,
        out_shape=[
            jax.ShapeDtypeStruct((inner, inner), F32),
            jax.ShapeDtypeStruct((width, inner), F32),
            jax.ShapeDtypeStruct((width, inner), F32),
            jax.ShapeDtypeStruct((nbasis, width), F32),
        ],
        scratch_shapes=[pltpu.VMEM((width, mine.shape[1]), F32)],
        compiler_params=limits(12),
        name="finish",
    )(*operands)


def swapped(value, axis, offset):
    return lax.ppermute(value, axis, [(i, i ^ offset) for i in range(lax.axis_size(axis))])


def groups_of(axis, first):
    low, groups = first, []
    while low < lax.axis_size(axis):
        members = min(4, lax.axis_size(axis) // low)
        groups.append((low, members))
        low *= members
    return groups


def total_of(parts):
    return sum(part.astype(F32) for part in parts).astype(BF16)


def scattered_sum(value, axis, low, members):
    digit = (lax.axis_index(axis) // low) % members
    rows = value.shape[0] // members

    def piece(k):
        return lax.dynamic_slice_in_dim(value, (digit ^ k) * rows, rows, 0)

    parts = [swapped(piece(k), axis, k * low) for k in range(members - 1, 0, -1)]
    return total_of([piece(0)] + parts)


def exchanged_sum(values, axis, low, members):
    parts = [[value] for value in values]
    for k in range(members - 1, 0, -1):
        for part, value in zip(parts, values):
            part.append(swapped(value, axis, k * low))
    return [total_of(part) for part in parts]


def shards(
    embed,
    cotangent,
    basis,
    triplet_row_index,
    triplet_slot_count,
    outgoing_edge_rows,
    residual_weight,
    down_weight,
    up_weight,
    basis_weight,
):
    rows, inner = embed.shape
    trips, nbasis = basis.shape[:2]

    pre, proj, *rest = project(embed, down_weight.T, outgoing_edge_rows)
    ghosts = pair_exchange(rest[:4])
    embed_v, down_v, outgoing_v = rest[4:]

    (cotangent_v, basis_v, index_v, count_v, up_v, bw_v, dres, mine, other) = residual(
        embed_v,
        residual_weight,
        cotangent,
        basis.reshape(trips * nbasis, rows),
        triplet_row_index,
        triplet_slot_count.reshape(1, rows),
        up_weight,
        basis_weight,
    )
    share = total_of([mine, swapped(other, "brick", 1)])
    slab_groups = groups_of("slab", 1)
    for low, members in reversed(slab_groups):
        share = scattered_sum(share, "slab", low, members)

    own, *terms, grads = triplets(
        proj, ghosts, basis_v, index_v, count_v, up_v, cotangent_v, bw_v
    )
    backs = pair_exchange(terms)
    dpre, mine, other = collect(own, backs, outgoing_v, pre, embed_v, grads)
    edge_grad = edge_gradient(dres, residual_weight, dpre, down_v)

    mine = total_of([mine, swapped(other, "brick", 1)])
    for low, members in groups_of("brick", 2):
        share, mine = exchanged_sum([share, mine], "brick", low, members)
    pieces = {0: share}
    for low, members in slab_groups:
        received = {}
        for k in range(members - 1, 0, -1):
            for offset, piece in pieces.items():
                received[offset ^ (k * low)] = swapped(piece, "slab", k * low)
        (mine,) = exchanged_sum([mine], "slab", low, members)
        pieces.update(received)
    sent = {offset: swapped(piece, "brick", 1) for offset, piece in pieces.items()}
    residual_grad, down_grad, up_grad, basis_grad = finish(
        pieces, sent, mine, swapped(mine, "brick", 1), inner, nbasis
    )
    return edge_grad, residual_grad, down_grad.T, up_grad, basis_grad


def solution(mesh):
    both = P(AXES, None)
    in_specs = (both, both, P(None, None, AXES), P(None, AXES), P(AXES), P(None, AXES)) + (P(),) * 4
    out_specs = (both, P(), P(), P(), P())
    return jax.shard_map(shards, mesh=mesh, in_specs=in_specs, out_specs=out_specs, check_vma=False)
```

```python
import jax
import jax.numpy as jnp
from jax import lax
from jax.experimental import pallas as pl
from jax.experimental.pallas import tpu as pltpu
from jax.sharding import PartitionSpec as P

AXES = ("slab", "brick")
LANES = 256
F32 = jnp.float32
BF16 = jnp.bfloat16
NN = ((1,), (0,))
NT = ((1,), (1,))
TN = ((0,), (0,))
VMEM = pl.BlockSpec(memory_space=pltpu.VMEM)
HBM = pl.BlockSpec(memory_space=pltpu.HBM)


def dot(a, b, dims, precision=None):
    return lax.dot_general(a, b, (dims, ((), ())), precision=precision, preferred_element_type=F32)


def like(*arrays):
    return [jax.ShapeDtypeStruct(a.shape, a.dtype) for a in arrays]


def in_hbm(*arrays):
    return [pltpu.with_memory_space_constraint(a, pltpu.HBM) for a in arrays]


def limits(mib):
    return pltpu.CompilerParams(vmem_limit_bytes=mib * 2**20)


def cost(flops):
    return pl.CostEstimate(flops=flops, bytes_accessed=0, transcendentals=0)


def in_vmem(*arrays):
    return [pltpu.VMEM(a.shape, a.dtype) for a in arrays]


def blocks_of(width):
    return [pl.ds(start, 128) for start in range(0, width, 128)]


def sigmoid(value):
    return 1.0 / (1.0 + jnp.exp(-value))


def silu_grad(value):
    sig = sigmoid(value)
    return sig * (1.0 + value * (1.0 - sig))


def parity(axis):
    return lax.axis_index(axis) % 2 == 1


def onehot(low):
    rows = lax.broadcasted_iota(jnp.int32, (LANES, low.shape[1]), 0).astype(jnp.int16)
    return jnp.where(rows == low.astype(jnp.int16), jnp.ones((), BF16), jnp.zeros((), BF16))


def stacked(table):
    return jnp.concatenate(
        [table[:, g * LANES : (g + 1) * LANES] for g in range(table.shape[1] // LANES)], axis=0
    )


def unstacked(blocks, width):
    return jnp.concatenate(
        [blocks[g * width : (g + 1) * width] for g in range(blocks.shape[0] // width)], axis=1
    )


def chosen(blocks, high, width):
    total = jnp.zeros((width, blocks.shape[1]), F32)
    for g in range(blocks.shape[0] // width):
        total = jnp.where(high == g, blocks[g * width : (g + 1) * width], total)
    return total


def spread(values, high, groups):
    zero = jnp.zeros_like(values)
    return jnp.concatenate([jnp.where(high == g, values, zero) for g in range(groups)], axis=0)


def pair_lists(rows_ref):
    lists = []
    for first, axis in ((0, "slab"), (2, "brick")):
        odd = parity(axis)
        up, down = rows_ref[first : first + 1, :], rows_ref[first + 1 : first + 2, :]
        lists += [jnp.where(odd, down, up), jnp.where(odd, up, down)]
    return lists


def paired(value, axis, first):
    count = lax.axis_size(axis)
    pairs = []
    for i in range(first, count, 2):
        j = (i + 1) % count
        pairs += [(i, j), (j, i)]
    return lax.ppermute(value, axis, pairs)


def pair_exchange(values):
    spots = (("slab", 0), ("slab", 1), ("brick", 0), ("brick", 1))
    sent = {k: paired(values[k], *spots[k]) for k in (3, 1, 0, 2)}
    return [sent[k] for k in range(4)]


def project_kernel(
    embed_ref, down_ref, rows_ref, pre_ref, proj_ref, s0, s1, s2, s3, embed_v, down_v, rows_v, sems
):
    copies = [
        pltpu.make_async_copy(source, target, sems.at[i])
        for i, (source, target) in enumerate(
            ((embed_ref, embed_v), (down_ref, down_v), (rows_ref, rows_v))
        )
    ]
    for copy in copies:
        copy.start()
    for copy in copies:
        copy.wait()
    pre = dot(down_v[...], embed_v[...], NT)
    pre_ref[...] = pre
    proj = (pre * sigmoid(pre)).astype(BF16)
    proj_ref[...] = proj
    table = stacked(proj)
    for index, send_ref in zip(pair_lists(rows_v), (s0, s1, s2, s3)):
        picked = dot(table, onehot(index & (LANES - 1)), NN)
        send_ref[...] = chosen(picked, index // LANES, proj.shape[0]).astype(BF16)


def project(embed, down_t, outgoing):
    rows, width = embed.shape[0], down_t.shape[0]
    ghost = jax.ShapeDtypeStruct((width, outgoing.shape[1]), BF16)
    return pl.pallas_call(
        project_kernel,
        in_specs=[HBM] * 3,
        out_specs=[VMEM] * 9,
        out_shape=[pltpu.VMEM((width, rows), F32), pltpu.VMEM((width, rows), BF16)]
        + in_vmem(*[ghost] * 4, embed, down_t, outgoing),
        scratch_shapes=[pltpu.SemaphoreType.DMA((3,))],
        compiler_params=limits(12),
        name="project",
    )(*in_hbm(embed, down_t, outgoing))


def residual_kernel(embed_ref, weight_ref, cotangent_ref, *refs):
    count = (len(refs) - 7) // 2
    sources, targets = refs[:count], refs[count : 2 * count]
    dres_ref, mine_ref, other_ref, cotangent_v, dres_v, grad_ref, sems = refs[2 * count :]
    rows = embed_ref.shape[0]
    block = min(rows, LANES)
    spans = [pl.ds(start, block) for start in range(0, rows, block)]
    reads = [
        pltpu.make_async_copy(cotangent_ref.at[at, :], cotangent_v.at[at, :], sems.at[i])
        for i, at in enumerate(spans)
    ]
    writes = [
        pltpu.make_async_copy(dres_v.at[at, :], dres_ref.at[at, :], sems.at[len(spans) + i])
        for i, at in enumerate(spans)
    ]
    copies = [
        pltpu.make_async_copy(source, target, sems.at[2 * len(spans) + i])
        for i, (source, target) in enumerate(zip(sources, targets))
    ]
    for copy in reads + copies:
        copy.start()
    for at, read, write in zip(spans, reads, writes):
        res_pre = dot(embed_ref[at, :], weight_ref[...], NN)
        grad = silu_grad(res_pre)
        read.wait()
        dres_v[at, :] = (cotangent_v[at, :].astype(F32) * grad).astype(BF16)
        write.start()
    grad_ref[...] = dot(embed_ref[...], dres_v[...], TN).astype(BF16)
    half = grad_ref.shape[0] // 2
    upper = lax.axis_index("brick") % 2
    columns = blocks_of(grad_ref.shape[1])
    step = half // lax.axis_size("slab")
    for part in range(half // step):
        for c, column in enumerate(columns):
            to = pl.ds((part * len(columns) + c) * step, step)
            mine_ref[to, :] = grad_ref[pl.ds(upper * half + part * step, step), column]
            other_ref[to, :] = grad_ref[pl.ds((1 - upper) * half + part * step, step), column]
    for copy in writes + copies:
        copy.wait()


def residual(embed, weight, cotangent, *staged):
    half = jax.ShapeDtypeStruct((weight.size // 256, 128), BF16)
    blocks = embed.shape[0] // min(embed.shape[0], LANES)
    return pl.pallas_call(
        residual_kernel,
        in_specs=[VMEM] * 2 + [HBM] * (1 + len(staged)),
        out_specs=[VMEM] * len(staged) + [HBM] + [VMEM] * 2,
        out_shape=in_vmem(*staged) + [pltpu.HBM(embed.shape, BF16)] + in_vmem(half, half),
        scratch_shapes=[
            pltpu.VMEM(embed.shape, BF16),
            pltpu.VMEM(embed.shape, BF16),
            pltpu.VMEM(weight.shape, BF16),
            pltpu.SemaphoreType.DMA((2 * blocks + len(staged),)),
        ],
        compiler_params=limits(16),
        cost_estimate=cost(6 * embed.size * weight.shape[1]),
        name="residual",
    )(embed, weight, *in_hbm(cotangent, *staged))


def triplet_kernel(
    proj_ref,
    g0_ref,
    g1_ref,
    g2_ref,
    g3_ref,
    index_ref,
    count_ref,
    up_ref,
    bw_ref,
    basis_hbm,
    cotangent_hbm,
    own_ref,
    t0_ref,
    t1_ref,
    t2_ref,
    t3_ref,
    grads_ref,
    table_ref,
    weight_ref,
    hot_ref,
    picked_ref,
    dw_ref,
    tsum_ref,
    dt_ref,
    acc_ref,
    basis_ref,
    cotangent_ref,
    sems,
):
    read_basis = pltpu.make_async_copy(basis_hbm, basis_ref, sems.at[0])
    read_cotangent = pltpu.make_async_copy(cotangent_hbm, cotangent_ref, sems.at[1])
    read_basis.start()
    read_cotangent.start()
    width, rows = proj_ref.shape
    trips = index_ref.shape[0]
    nbasis = bw_ref.shape[0]
    own_groups = rows // LANES
    blocks = []
    for a_ref, b_ref, axis in ((g0_ref, g1_ref, "slab"), (g2_ref, g3_ref, "brick")):
        odd = parity(axis)
        a, b = a_ref[...], b_ref[...]
        blocks += [jnp.where(odd, a, b), jnp.where(odd, b, a)]
    table_ref[: own_groups * width, :] = stacked(proj_ref[...])
    table_ref[own_groups * width :, :] = stacked(jnp.concatenate(blocks, axis=1))
    groups = table_ref.shape[0] // width
    tiles = rows // LANES

    span = trips * nbasis
    fold = jnp.where(
        lax.broadcasted_iota(jnp.int32, (nbasis, span), 1) % nbasis
        == lax.broadcasted_iota(jnp.int32, (nbasis, span), 0),
        1.0,
        0.0,
    )
    wide = dot(bw_ref[...], fold.astype(BF16), TN).astype(BF16)
    own_slot = lax.broadcasted_iota(jnp.int32, (trips, width, span), 0) == (
        lax.broadcasted_iota(jnp.int32, (trips, width, span), 2) // nbasis
    )
    diagonal = jnp.where(own_slot, wide[None], jnp.zeros((), BF16)).reshape(trips * width, span)
    read_basis.wait()
    weight_ref[...] = dot(diagonal, basis_ref[...], NN)

    tsum_ref[...] = jnp.zeros_like(tsum_ref)

    def lookup(j, t):
        at = pl.ds(t * LANES, LANES)
        index = index_ref[pl.ds(j, 1), at]
        high = jnp.where(j < count_ref[:, at], index // LANES, -1)
        return at, index & (LANES - 1), high

    def forward(j, carry):
        for t in range(tiles):
            at, low, high = lookup(j, t)
            hot = onehot(low)
            hot_ref[j, :, at] = hot
            picked = chosen(dot(table_ref[...], hot, NN), high, width)
            picked_ref[j, :, at] = picked.astype(BF16)
            tsum_ref[:, at] += weight_ref[pl.ds(j * width, width), at] * picked
        return carry

    lax.fori_loop(0, trips, forward, 0, unroll=8)

    tsum = tsum_ref[...]
    sig = sigmoid(tsum)
    act = (tsum * sig).astype(BF16)
    read_cotangent.wait()
    cotangent = cotangent_ref[...]
    inner = cotangent.shape[1]
    grads_ref[:, :inner] = dot(act, cotangent, NN).astype(BF16)
    dsum = dot(up_ref[...], cotangent, NT)
    dt_ref[...] = dsum * (sig * (1.0 + tsum * (1.0 - sig)))
    acc_ref[...] = jnp.zeros_like(acc_ref)

    def backward(j, carry):
        parts = []
        for t in range(tiles):
            at, low, high = lookup(j, t)
            dt = dt_ref[:, at]
            dw_ref[pl.ds(j * width, width), at] = (dt * picked_ref[j, :, at].astype(F32)).astype(BF16)
            terms = (dt * weight_ref[pl.ds(j * width, width), at]).astype(BF16)
            parts.append(spread(terms, high, groups))
        acc_ref[...] += dot(jnp.concatenate(parts, axis=1), hot_ref[j], NT)
        return carry

    lax.fori_loop(0, trips, backward, 0, unroll=8)

    own_ref[...] = unstacked(acc_ref[: own_groups * width, :], width)
    ghost_terms = unstacked(acc_ref[own_groups * width :, :], width).astype(BF16)
    ghost = t0_ref.shape[1]
    for first, axis, a_ref, b_ref in ((0, "slab", t0_ref, t1_ref), (2, "brick", t2_ref, t3_ref)):
        odd = parity(axis)
        prev = ghost_terms[:, first * ghost : (first + 1) * ghost]
        following = ghost_terms[:, (first + 1) * ghost : (first + 2) * ghost]
        a_ref[...] = jnp.where(odd, prev, following)
        b_ref[...] = jnp.where(odd, following, prev)
    full = dot(dw_ref[...], basis_ref[...], NT).reshape(trips, width, span)
    kept = jnp.sum(jnp.where(own_slot, full, 0.0), axis=0)
    folded = dot(kept, fold, NT, lax.Precision.HIGHEST)
    pad = grads_ref.shape[1] - inner - nbasis
    grads_ref[:, inner:] = jnp.concatenate(
        [folded, jnp.zeros((width, pad), F32)], axis=1
    ).astype(BF16)


def triplets(proj, ghosts, basis, index, count, up_weight, cotangent, basis_weight):
    width, rows = proj.shape
    trips = index.shape[0]
    ghost = ghosts[0].shape[1]
    inner = cotangent.shape[1]
    groups = (rows + 4 * ghost) // LANES
    operands = (proj, *ghosts, index, count, up_weight, basis_weight)
    out_shape = (
        [pltpu.VMEM((width, rows), F32)]
        + in_vmem(*ghosts)
        + [pltpu.VMEM((width, inner + 128), BF16)]
    )
    return pl.pallas_call(
        triplet_kernel,
        in_specs=[VMEM] * len(operands) + [HBM] * 2,
        out_specs=[VMEM] * len(out_shape),
        out_shape=out_shape,
        scratch_shapes=[
            pltpu.VMEM((groups * width, LANES), BF16),
            pltpu.VMEM((trips * width, rows), F32),
            pltpu.VMEM((trips, LANES, rows), BF16),
            pltpu.VMEM((trips, width, rows), BF16),
            pltpu.VMEM((trips * width, rows), BF16),
            pltpu.VMEM((width, rows), F32),
            pltpu.VMEM((width, rows), F32),
            pltpu.VMEM((groups * width, LANES), F32),
            pltpu.VMEM(basis.shape, BF16),
            pltpu.VMEM(cotangent.shape, BF16),
            pltpu.SemaphoreType.DMA((2,)),
        ],
        compiler_params=limits(28),
        cost_estimate=cost(8 * trips * rows * width * (rows + 4 * ghost)),
        name="triplets",
    )(*operands, *in_hbm(basis, cotangent))


def collect_kernel(
    own_ref,
    b0_ref,
    b1_ref,
    b2_ref,
    b3_ref,
    rows_ref,
    pre_ref,
    embed_ref,
    grads_ref,
    dpre_ref,
    mine_ref,
    other_ref,
    all_ref,
):
    width, rows = own_ref.shape
    groups = rows // LANES
    acc = jnp.zeros((groups * width, LANES), F32)
    for index, back_ref in zip(pair_lists(rows_ref), (b0_ref, b1_ref, b2_ref, b3_ref)):
        acc += dot(spread(back_ref[...], index // LANES, groups), onehot(index & (LANES - 1)), NT)
    dproj = own_ref[...] + unstacked(acc, width)
    dpre = (dproj * silu_grad(pre_ref[...])).astype(BF16)
    dpre_ref[...] = dpre
    inner = embed_ref.shape[1]
    all_ref[:, :inner] = dot(dpre, embed_ref[...], NN).astype(BF16)
    all_ref[:, inner:] = grads_ref[...]
    half = width // 2
    upper = lax.axis_index("brick") % 2
    for c, column in enumerate(blocks_of(all_ref.shape[1])):
        to = pl.ds(c * half, half)
        mine_ref[to, :] = all_ref[pl.ds(upper * half, half), column]
        other_ref[to, :] = all_ref[pl.ds((1 - upper) * half, half), column]


def collect(own, backs, outgoing, pre, embed, grads):
    width = own.shape[0]
    total = embed.shape[1] + grads.shape[1]
    half = pltpu.VMEM((width * total // 256, 128), BF16)
    operands = (own, *backs, outgoing, pre, embed, grads)
    return pl.pallas_call(
        collect_kernel,
        in_specs=[VMEM] * len(operands),
        out_specs=[VMEM] * 3,
        out_shape=[pltpu.VMEM(own.shape, BF16), half, half],
        scratch_shapes=[pltpu.VMEM((width, total), BF16)],
        compiler_params=limits(12),
        name="collect",
    )(*operands)


def edge_kernel(weight_ref, dpre_ref, down_ref, dres_hbm, out_ref, dres_ref, sems):
    rows = dres_ref.shape[0]
    block = min(rows, LANES)
    spans = [pl.ds(start, block) for start in range(0, rows, block)]
    reads = [
        pltpu.make_async_copy(dres_hbm.at[at, :], dres_ref.at[at, :], sems.at[i])
        for i, at in enumerate(spans)
    ]
    for read in reads:
        read.start()
    for at, read in zip(spans, reads):
        down_term = dot(dpre_ref[:, at], down_ref[...], TN)
        read.wait()
        out_ref[at, :] = (dot(dres_ref[at, :], weight_ref[...], NT) + down_term).astype(BF16)


def edge_gradient(dres, weight, dpre, down_t):
    rows, inner = dres.shape
    return pl.pallas_call(
        edge_kernel,
        in_specs=[VMEM] * 3 + [HBM],
        out_specs=VMEM,
        out_shape=jax.ShapeDtypeStruct((rows, inner), BF16),
        scratch_shapes=[
            pltpu.VMEM((rows, inner), BF16),
            pltpu.SemaphoreType.DMA((rows // min(rows, LANES),)),
        ],
        compiler_params=limits(12),
        cost_estimate=cost(4 * rows * inner * (inner + down_t.shape[0])),
        name="edge_gradient",
    )(weight, dpre, down_t, *in_hbm(dres))


def finish_kernel(offsets, mine_ref, other_ref, residual_ref, down_ref, up_ref, basis_ref, all_ref):
    upper = lax.axis_index("brick") % 2
    slab = lax.axis_index("slab")
    rows, inner = all_ref.shape[0] // 2, down_ref.shape[1]
    half = residual_ref.shape[0] // 2
    step = half // len(offsets)
    columns = blocks_of(residual_ref.shape[1])
    for source, side in ((mine_ref, upper), (other_ref, 1 - upper)):
        for c, column in enumerate(blocks_of(all_ref.shape[1])):
            all_ref[pl.ds(side * rows, rows), column] = source[pl.ds(c * rows, rows), :].astype(F32)
        first = rows * all_ref.shape[1] // 128
        for i, offset in enumerate(offsets):
            place = pl.ds(side * half + (slab ^ offset) * step, step)
            for c, column in enumerate(columns):
                at = pl.ds(first + (i * len(columns) + c) * step, step)
                residual_ref[place, column] = source[at, :].astype(F32)
    down_ref[...] = all_ref[:, :inner]
    up_ref[...] = all_ref[:, inner : 2 * inner]
    basis_ref[...] = all_ref[:, 2 * inner :].T[: basis_ref.shape[0], :]


def finish(offsets, mine, other, inner, width, nbasis):
    return pl.pallas_call(
        lambda *refs: finish_kernel(offsets, *refs),
        in_specs=[VMEM] * 2,
        out_specs=[VMEM] * 4,
        out_shape=[
            jax.ShapeDtypeStruct((inner, inner), F32),
            jax.ShapeDtypeStruct((width, inner), F32),
            jax.ShapeDtypeStruct((width, inner), F32),
            jax.ShapeDtypeStruct((nbasis, width), F32),
        ],
        scratch_shapes=[pltpu.VMEM((width, 2 * inner + 128), F32)],
        compiler_params=limits(12),
        name="finish",
    )(mine, other)


def swapped(value, axis, offset):
    return lax.ppermute(value, axis, [(i, i ^ offset) for i in range(lax.axis_size(axis))])


def groups_of(axis, first):
    low, groups = first, []
    while low < lax.axis_size(axis):
        members = min(4, lax.axis_size(axis) // low)
        groups.append((low, members))
        low *= members
    return groups


def total_of(parts):
    return sum(part.astype(F32) for part in parts).astype(BF16)


def scattered_sum(value, axis, low, members):
    digit = (lax.axis_index(axis) // low) % members
    rows = value.shape[0] // members

    def piece(k):
        return lax.dynamic_slice_in_dim(value, (digit ^ k) * rows, rows, 0)

    parts = [swapped(piece(k), axis, k * low) for k in range(members - 1, 0, -1)]
    return total_of([piece(0)] + parts)


def exchanged(value, axis, low, members):
    return {k * low: swapped(value, axis, k * low) for k in range(members - 1, 0, -1)}


def shards(
    embed,
    cotangent,
    basis,
    triplet_row_index,
    triplet_slot_count,
    outgoing_edge_rows,
    residual_weight,
    down_weight,
    up_weight,
    basis_weight,
):
    rows, inner = embed.shape
    trips, nbasis = basis.shape[:2]

    pre, proj, *rest = project(embed, down_weight.T, outgoing_edge_rows)
    ghosts = pair_exchange(rest[:4])
    embed_v, down_v, outgoing_v = rest[4:]

    index_v, count_v, up_v, bw_v, dres, mine, other = residual(
        embed_v,
        residual_weight,
        cotangent,
        triplet_row_index,
        triplet_slot_count.reshape(1, rows),
        up_weight,
        basis_weight,
    )
    share = total_of([mine, swapped(other, "brick", 1)])

    own, *terms, grads = triplets(
        proj,
        ghosts,
        basis.reshape(trips * nbasis, rows),
        index_v,
        count_v,
        up_v,
        cotangent,
        bw_v,
    )
    *terms, share = lax.optimization_barrier((*terms, share))
    backs = pair_exchange(terms)
    slab_groups = groups_of("slab", 1)
    for low, members in reversed(slab_groups):
        share = scattered_sum(share, "slab", low, members)
    *backs, share = lax.optimization_barrier((*backs, share))
    dpre, mine, other = collect(own, backs, outgoing_v, pre, embed_v, grads)

    mine = total_of([mine, swapped(other, "brick", 1)])
    mine, dpre = lax.optimization_barrier((mine, dpre))
    edge_grad = edge_gradient(dres, residual_weight, dpre, down_v)
    count = mine.shape[0]
    value = jnp.concatenate([mine, share], axis=0)
    for low, members in groups_of("brick", 2):
        value = total_of([value, *exchanged(value, "brick", low, members).values()])
    value, edge_grad = lax.optimization_barrier((value, edge_grad))
    pieces = {0: value[count:]}
    for low, members in slab_groups:
        received = exchanged(value, "slab", low, members)
        mine = total_of([value[:count]] + [other[:count] for other in received.values()])
        known = sorted(pieces)
        step = share.shape[0]
        for k, other in received.items():
            for i, offset in enumerate(known):
                pieces[offset ^ k] = other[count + i * step : count + (i + 1) * step]
        value = jnp.concatenate([mine] + [pieces[o] for o in sorted(pieces)], axis=0)
    residual_grad, down_grad, up_grad, basis_grad = finish(
        sorted(pieces), value, swapped(value, "brick", 1), inner, proj.shape[0], nbasis
    )
    return edge_grad, residual_grad, down_grad.T, up_grad, basis_grad


def solution(mesh):
    both = P(AXES, None)
    in_specs = (both, both, P(None, None, AXES), P(None, AXES), P(AXES), P(None, AXES)) + (P(),) * 4
    out_specs = (both, P(), P(), P(), P())
    return jax.shard_map(shards, mesh=mesh, in_specs=in_specs, out_specs=out_specs, check_vma=False)
```

```python
import jax
import jax.numpy as jnp
from jax import lax
from jax.experimental import pallas as pl
from jax.experimental.pallas import tpu as pltpu
from jax.sharding import PartitionSpec as P

AXES = ("slab", "brick")
LANES = 256
F32 = jnp.float32
BF16 = jnp.bfloat16
NN = ((1,), (0,))
NT = ((1,), (1,))
TN = ((0,), (0,))
VMEM = pl.BlockSpec(memory_space=pltpu.VMEM)
HBM = pl.BlockSpec(memory_space=pltpu.HBM)


def dot(a, b, dims, precision=None):
    return lax.dot_general(a, b, (dims, ((), ())), precision=precision, preferred_element_type=F32)


def like(*arrays):
    return [jax.ShapeDtypeStruct(a.shape, a.dtype) for a in arrays]


def in_hbm(*arrays):
    return [pltpu.with_memory_space_constraint(a, pltpu.HBM) for a in arrays]


def limits(mib):
    return pltpu.CompilerParams(vmem_limit_bytes=mib * 2**20)


def cost(flops):
    return pl.CostEstimate(flops=flops, bytes_accessed=0, transcendentals=0)


def in_vmem(*arrays):
    return [pltpu.VMEM(a.shape, a.dtype) for a in arrays]


def blocks_of(width):
    return [pl.ds(start, 128) for start in range(0, width, 128)]


def sigmoid(value):
    return 1.0 / (1.0 + jnp.exp(-value))


def silu_grad(value):
    sig = sigmoid(value)
    return sig * (1.0 + value * (1.0 - sig))


def parity(axis):
    return lax.axis_index(axis) % 2 == 1


def onehot(low):
    rows = lax.broadcasted_iota(jnp.int32, (LANES, low.shape[1]), 0).astype(jnp.int16)
    return jnp.where(rows == low.astype(jnp.int16), jnp.ones((), BF16), jnp.zeros((), BF16))


def stacked(table):
    return jnp.concatenate(
        [table[:, g * LANES : (g + 1) * LANES] for g in range(table.shape[1] // LANES)], axis=0
    )


def unstacked(blocks, width):
    return jnp.concatenate(
        [blocks[g * width : (g + 1) * width] for g in range(blocks.shape[0] // width)], axis=1
    )


def chosen(blocks, high, width):
    total = jnp.zeros((width, blocks.shape[1]), F32)
    for g in range(blocks.shape[0] // width):
        total = jnp.where(high == g, blocks[g * width : (g + 1) * width], total)
    return total


def spread(values, high, groups):
    zero = jnp.zeros_like(values)
    return jnp.concatenate([jnp.where(high == g, values, zero) for g in range(groups)], axis=0)


def pair_lists(rows_ref):
    lists = []
    for first, axis in ((0, "slab"), (2, "brick")):
        odd = parity(axis)
        up, down = rows_ref[first : first + 1, :], rows_ref[first + 1 : first + 2, :]
        lists += [jnp.where(odd, down, up), jnp.where(odd, up, down)]
    return lists


def paired(value, axis, first):
    count = lax.axis_size(axis)
    pairs = []
    for i in range(first, count, 2):
        j = (i + 1) % count
        pairs += [(i, j), (j, i)]
    return lax.ppermute(value, axis, pairs)


def pair_exchange(values):
    spots = (("slab", 0), ("slab", 1), ("brick", 0), ("brick", 1))
    sent = {k: paired(values[k], *spots[k]) for k in (3, 1, 0, 2)}
    return [sent[k] for k in range(4)]


def select_kernel(embed_ref, rows_ref, s0, s1, s2, s3, embed_v, rows_v, sems):
    copies = [
        pltpu.make_async_copy(rows_ref, rows_v, sems.at[0]),
        pltpu.make_async_copy(embed_ref, embed_v, sems.at[1]),
    ]
    for copy in copies:
        copy.start()
    for copy in copies:
        copy.wait()
    rows = embed_v.shape[0]
    for index, send_ref in zip(pair_lists(rows_v), (s0, s1, s2, s3)):
        spots = lax.broadcasted_iota(jnp.int32, (rows, index.shape[1]), 0).astype(jnp.int16)
        hot = jnp.where(spots == index.astype(jnp.int16), jnp.ones((), BF16), jnp.zeros((), BF16))
        send_ref[...] = dot(hot, embed_v[...], TN).astype(BF16)


def select(embed, outgoing):
    ghost = jax.ShapeDtypeStruct((outgoing.shape[1], embed.shape[1]), BF16)
    return pl.pallas_call(
        select_kernel,
        in_specs=[HBM] * 2,
        out_specs=[VMEM] * 6,
        out_shape=in_vmem(*[ghost] * 4, embed, outgoing),
        scratch_shapes=[pltpu.SemaphoreType.DMA((2,))],
        compiler_params=limits(12),
        name="select",
    )(*in_hbm(embed, outgoing))


def residual_kernel(embed_ref, weight_ref, cotangent_ref, *refs):
    count = (len(refs) - 9) // 2
    sources, targets = refs[:count], refs[count : 2 * count]
    dres_ref, mine_ref, other_ref, pre_ref, proj_ref = refs[2 * count : 2 * count + 5]
    cotangent_v, dres_v, grad_ref, sems = refs[2 * count + 5 :]
    rows = embed_ref.shape[0]
    block = min(rows, LANES)
    spans = [pl.ds(start, block) for start in range(0, rows, block)]
    reads = [
        pltpu.make_async_copy(cotangent_ref.at[at, :], cotangent_v.at[at, :], sems.at[i])
        for i, at in enumerate(spans)
    ]
    writes = [
        pltpu.make_async_copy(dres_v.at[at, :], dres_ref.at[at, :], sems.at[len(spans) + i])
        for i, at in enumerate(spans)
    ]
    copies = [
        pltpu.make_async_copy(source, target, sems.at[2 * len(spans) + i])
        for i, (source, target) in enumerate(zip(sources, targets))
    ]
    for copy in reads + copies:
        copy.start()
    for at, read, write in zip(spans, reads, writes):
        res_pre = dot(embed_ref[at, :], weight_ref[...], NN)
        grad = silu_grad(res_pre)
        read.wait()
        dres_v[at, :] = (cotangent_v[at, :].astype(F32) * grad).astype(BF16)
        write.start()
    copies[0].wait()
    pre = dot(targets[0][...], embed_ref[...], NT)
    pre_ref[...] = pre
    proj_ref[...] = (pre * sigmoid(pre)).astype(BF16)
    grad_ref[...] = dot(embed_ref[...], dres_v[...], TN).astype(BF16)
    half = grad_ref.shape[0] // 2
    upper = lax.axis_index("brick") % 2
    columns = blocks_of(grad_ref.shape[1])
    step = half // lax.axis_size("slab")
    for part in range(half // step):
        for c, column in enumerate(columns):
            to = pl.ds((part * len(columns) + c) * step, step)
            mine_ref[to, :] = grad_ref[pl.ds(upper * half + part * step, step), column]
            other_ref[to, :] = grad_ref[pl.ds((1 - upper) * half + part * step, step), column]
    for copy in writes + copies[1:]:
        copy.wait()


def residual(embed, weight, cotangent, down_t, *staged):
    staged = (down_t, *staged)
    width, rows = down_t.shape[0], embed.shape[0]
    half = jax.ShapeDtypeStruct((weight.size // 256, 128), BF16)
    blocks = embed.shape[0] // min(embed.shape[0], LANES)
    return pl.pallas_call(
        residual_kernel,
        in_specs=[VMEM] * 2 + [HBM] * (1 + len(staged)),
        out_specs=[VMEM] * len(staged) + [HBM] + [VMEM] * 4,
        out_shape=in_vmem(*staged)
        + [pltpu.HBM(embed.shape, BF16)]
        + in_vmem(half, half)
        + [pltpu.VMEM((width, rows), F32), pltpu.VMEM((width, rows), BF16)],
        scratch_shapes=[
            pltpu.VMEM(embed.shape, BF16),
            pltpu.VMEM(embed.shape, BF16),
            pltpu.VMEM(weight.shape, BF16),
            pltpu.SemaphoreType.DMA((2 * blocks + len(staged),)),
        ],
        compiler_params=limits(16),
        cost_estimate=cost(6 * embed.size * weight.shape[1]),
        name="residual",
    )(embed, weight, *in_hbm(cotangent, *staged))


def triplet_kernel(
    proj_ref,
    pre_ref,
    embed_ref,
    down_ref,
    g0_ref,
    g1_ref,
    g2_ref,
    g3_ref,
    index_ref,
    count_ref,
    up_ref,
    bw_ref,
    basis_hbm,
    cotangent_hbm,
    own_ref,
    t0_ref,
    t1_ref,
    t3_ref,
    mine_ref,
    other_ref,
    ghost_embed_ref,
    rest_ref,
    table_ref,
    weight_ref,
    hot_ref,
    picked_ref,
    dw_ref,
    tsum_ref,
    dt_ref,
    acc_ref,
    basis_ref,
    cotangent_ref,
    sems,
):
    read_basis = pltpu.make_async_copy(basis_hbm, basis_ref, sems.at[0])
    read_cotangent = pltpu.make_async_copy(cotangent_hbm, cotangent_ref, sems.at[1])
    read_basis.start()
    read_cotangent.start()
    width, rows = proj_ref.shape
    trips = index_ref.shape[0]
    nbasis = bw_ref.shape[0]
    own_groups = rows // LANES
    ghost = g0_ref.shape[0]
    for first, a_ref, b_ref, axis in ((0, g0_ref, g1_ref, "slab"), (2, g2_ref, g3_ref, "brick")):
        odd = parity(axis)
        a, b = a_ref[...], b_ref[...]
        ghost_embed_ref[first * ghost : (first + 1) * ghost, :] = jnp.where(odd, a, b)
        ghost_embed_ref[(first + 1) * ghost : (first + 2) * ghost, :] = jnp.where(odd, b, a)
    ghost_pre = dot(down_ref[...], ghost_embed_ref[...], NT)
    ghost_grad = silu_grad(ghost_pre)
    table_ref[: own_groups * width, :] = stacked(proj_ref[...])
    table_ref[own_groups * width :, :] = stacked((ghost_pre * sigmoid(ghost_pre)).astype(BF16))
    groups = table_ref.shape[0] // width
    tiles = rows // LANES

    span = trips * nbasis
    fold = jnp.where(
        lax.broadcasted_iota(jnp.int32, (nbasis, span), 1) % nbasis
        == lax.broadcasted_iota(jnp.int32, (nbasis, span), 0),
        1.0,
        0.0,
    )
    wide = dot(bw_ref[...], fold.astype(BF16), TN).astype(BF16)
    own_slot = lax.broadcasted_iota(jnp.int32, (trips, width, span), 0) == (
        lax.broadcasted_iota(jnp.int32, (trips, width, span), 2) // nbasis
    )
    diagonal = jnp.where(own_slot, wide[None], jnp.zeros((), BF16)).reshape(trips * width, span)
    read_basis.wait()
    weight_ref[...] = dot(diagonal, basis_ref[...], NN)

    tsum_ref[...] = jnp.zeros_like(tsum_ref)

    def lookup(j, t):
        at = pl.ds(t * LANES, LANES)
        index = index_ref[pl.ds(j, 1), at]
        high = jnp.where(j < count_ref[:, at], index // LANES, -1)
        return at, index & (LANES - 1), high

    def forward(j, carry):
        for t in range(tiles):
            at, low, high = lookup(j, t)
            hot = onehot(low)
            hot_ref[j, :, at] = hot
            picked = chosen(dot(table_ref[...], hot, NN), high, width)
            picked_ref[j, :, at] = picked.astype(BF16)
            tsum_ref[:, at] += weight_ref[pl.ds(j * width, width), at] * picked
        return carry

    lax.fori_loop(0, trips, forward, 0, unroll=8)

    tsum = tsum_ref[...]
    sig = sigmoid(tsum)
    act = (tsum * sig).astype(BF16)
    read_cotangent.wait()
    cotangent = cotangent_ref[...]
    inner = cotangent.shape[1]
    rest_ref[:, inner : 2 * inner] = dot(act, cotangent, NN).astype(BF16)
    dsum = dot(up_ref[...], cotangent, NT)
    dt_ref[...] = dsum * (sig * (1.0 + tsum * (1.0 - sig)))
    acc_ref[...] = jnp.zeros_like(acc_ref)

    def backward(j, carry):
        parts = []
        for t in range(tiles):
            at, low, high = lookup(j, t)
            dt = dt_ref[:, at]
            dw_ref[pl.ds(j * width, width), at] = (dt * picked_ref[j, :, at].astype(F32)).astype(BF16)
            terms = (dt * weight_ref[pl.ds(j * width, width), at]).astype(BF16)
            parts.append(spread(terms, high, groups))
        acc_ref[...] += dot(jnp.concatenate(parts, axis=1), hot_ref[j], NT)
        return carry

    lax.fori_loop(0, trips, backward, 0, unroll=8)

    own = unstacked(acc_ref[: own_groups * width, :], width)
    own_ref[...] = own
    ghost_terms = unstacked(acc_ref[own_groups * width :, :], width)
    sides = []
    for first, axis in ((0, "slab"), (2, "brick")):
        odd = parity(axis)
        prev = ghost_terms[:, first * ghost : (first + 1) * ghost].astype(BF16)
        following = ghost_terms[:, (first + 1) * ghost : (first + 2) * ghost].astype(BF16)
        sides += [jnp.where(odd, prev, following), jnp.where(odd, following, prev)]
    t0_ref[...], t1_ref[...], t3_ref[...] = sides[0], sides[1], sides[3]
    down_grad = dot((own * silu_grad(pre_ref[...])).astype(BF16), embed_ref[...], NN)
    down_grad += dot((ghost_terms * ghost_grad).astype(BF16), ghost_embed_ref[...], NN)
    rest_ref[:, :inner] = down_grad.astype(BF16)
    full = dot(dw_ref[...], basis_ref[...], NT).reshape(trips, width, span)
    kept = jnp.sum(jnp.where(own_slot, full, 0.0), axis=0)
    folded = dot(kept, fold, NT, lax.Precision.HIGHEST)
    pad = rest_ref.shape[1] - 2 * inner - nbasis
    rest_ref[:, 2 * inner :] = jnp.concatenate(
        [folded, jnp.zeros((width, pad), F32)], axis=1
    ).astype(BF16)
    half = width // 2
    upper = lax.axis_index("brick") % 2
    columns = blocks_of(rest_ref.shape[1])
    for c, column in enumerate(columns):
        to = pl.ds(c * half, half)
        mine_ref[to, :] = rest_ref[pl.ds(upper * half, half), column]
        other_ref[to, :] = rest_ref[pl.ds((1 - upper) * half, half), column]
    used, total = len(columns) * half, mine_ref.shape[0]
    if used < total:
        mine_ref[used:, :] = jnp.zeros((total - used, 128), BF16)
        other_ref[used:total, :] = jnp.zeros((total - used, 128), BF16)
    for c, column in enumerate(blocks_of(ghost)):
        other_ref[pl.ds(total + c * width, width), :] = sides[2][:, column]


def triplets(
    proj, pre, embed, down_t, ghosts, basis, index, count, up_weight, cotangent, basis_weight
):
    width, rows = proj.shape
    trips = index.shape[0]
    ghost, inner = ghosts[0].shape
    groups = (rows + 4 * ghost) // LANES
    operands = (proj, pre, embed, down_t, *ghosts, index, count, up_weight, basis_weight)
    unit = 16 * lax.axis_size("slab")
    total = 2 * inner + 128
    shared = -(-(width * total // 256) // unit) * unit
    out_shape = (
        [pltpu.VMEM((width, rows), F32)]
        + [pltpu.VMEM((width, ghost), BF16)] * 3
        + [pltpu.VMEM((shared, 128), BF16), pltpu.VMEM((shared + width * ghost // 128, 128), BF16)]
    )
    return pl.pallas_call(
        triplet_kernel,
        in_specs=[VMEM] * len(operands) + [HBM] * 2,
        out_specs=[VMEM] * len(out_shape),
        out_shape=out_shape,
        scratch_shapes=[
            pltpu.VMEM((4 * ghost, inner), BF16),
            pltpu.VMEM((width, total), BF16),
            pltpu.VMEM((groups * width, LANES), BF16),
            pltpu.VMEM((trips * width, rows), F32),
            pltpu.VMEM((trips, LANES, rows), BF16),
            pltpu.VMEM((trips, width, rows), BF16),
            pltpu.VMEM((trips * width, rows), BF16),
            pltpu.VMEM((width, rows), F32),
            pltpu.VMEM((width, rows), F32),
            pltpu.VMEM((groups * width, LANES), F32),
            pltpu.VMEM(basis.shape, BF16),
            pltpu.VMEM(cotangent.shape, BF16),
            pltpu.SemaphoreType.DMA((2,)),
        ],
        compiler_params=limits(28),
        cost_estimate=cost(8 * trips * rows * width * (rows + 4 * ghost)),
        name="triplets",
    )(*operands, *in_hbm(basis, cotangent))


def edge_kernel(
    own_ref,
    b0_ref,
    b1_ref,
    b2_ref,
    b3_ref,
    rows_ref,
    pre_ref,
    weight_ref,
    down_ref,
    dres_hbm,
    out_ref,
    dres_ref,
    sems,
):
    width, rows = own_ref.shape
    block = min(rows, LANES)
    spans = [pl.ds(start, block) for start in range(0, rows, block)]
    reads = [
        pltpu.make_async_copy(dres_hbm.at[at, :], dres_ref.at[at, :], sems.at[i])
        for i, at in enumerate(spans)
    ]
    for read in reads:
        read.start()
    groups = rows // LANES
    acc = jnp.zeros((groups * width, LANES), F32)
    for index, back_ref in zip(pair_lists(rows_ref), (b0_ref, b1_ref, b2_ref, b3_ref)):
        acc += dot(spread(back_ref[...], index // LANES, groups), onehot(index & (LANES - 1)), NT)
    dproj = own_ref[...] + unstacked(acc, width)
    dpre = (dproj * silu_grad(pre_ref[...])).astype(BF16)
    for i, (at, read) in enumerate(zip(spans, reads)):
        down_term = dot(dpre[:, i * block : (i + 1) * block], down_ref[...], TN)
        read.wait()
        out_ref[at, :] = (dot(dres_ref[at, :], weight_ref[...], NT) + down_term).astype(BF16)


def edge_gradient(own, backs, outgoing, pre, weight, down_t, dres):
    rows, inner = dres.shape
    operands = (own, *backs, outgoing, pre, weight, down_t)
    return pl.pallas_call(
        edge_kernel,
        in_specs=[VMEM] * len(operands) + [HBM],
        out_specs=VMEM,
        out_shape=jax.ShapeDtypeStruct((rows, inner), BF16),
        scratch_shapes=[
            pltpu.VMEM((rows, inner), BF16),
            pltpu.SemaphoreType.DMA((rows // min(rows, LANES),)),
        ],
        compiler_params=limits(12),
        cost_estimate=cost(4 * rows * inner * (inner + down_t.shape[0])),
        name="edge_gradient",
    )(*operands, *in_hbm(dres))


def finish_kernel(
    offsets, mine_ref, other_ref, residual_ref, down_ref, up_ref, basis_ref, all_ref, part_ref
):
    upper = lax.axis_index("brick") % 2
    slab = lax.axis_index("slab")
    half = residual_ref.shape[0] // 2
    step = half // len(offsets)
    columns = blocks_of(residual_ref.shape[1])
    block = mine_ref.shape[0] // len(offsets)
    tail = len(columns) * step
    share = block - tail
    for source, side in ((mine_ref, upper), (other_ref, 1 - upper)):
        for i, offset in enumerate(offsets):
            place = pl.ds(side * half + (slab ^ offset) * step, step)
            for c, column in enumerate(columns):
                at = pl.ds(i * block + c * step, step)
                residual_ref[place, column] = source[at, :].astype(F32)
            place = pl.ds((side * len(offsets) + (slab ^ offset)) * share, share)
            part_ref[place, :] = source[pl.ds(i * block + tail, share), :].astype(F32)
    rows, inner = all_ref.shape[0] // 2, down_ref.shape[1]
    for side in range(2):
        for c, column in enumerate(blocks_of(all_ref.shape[1])):
            at = pl.ds(side * len(offsets) * share + c * rows, rows)
            all_ref[pl.ds(side * rows, rows), column] = part_ref[at, :]
    down_ref[...] = all_ref[:, :inner]
    up_ref[...] = all_ref[:, inner : 2 * inner]
    basis_ref[...] = all_ref[:, 2 * inner :].T[: basis_ref.shape[0], :]


def finish(offsets, mine, other, shared, inner, width, nbasis):
    return pl.pallas_call(
        lambda *refs: finish_kernel(offsets, *refs),
        in_specs=[VMEM] * 2,
        out_specs=[VMEM] * 4,
        out_shape=[
            jax.ShapeDtypeStruct((inner, inner), F32),
            jax.ShapeDtypeStruct((width, inner), F32),
            jax.ShapeDtypeStruct((width, inner), F32),
            jax.ShapeDtypeStruct((nbasis, width), F32),
        ],
        scratch_shapes=[
            pltpu.VMEM((width, 2 * inner + 128), F32),
            pltpu.VMEM((2 * shared, 128), F32),
        ],
        compiler_params=limits(12),
        name="finish",
    )(mine, other)


def swapped(value, axis, offset):
    return lax.ppermute(value, axis, [(i, i ^ offset) for i in range(lax.axis_size(axis))])


def groups_of(axis, first):
    low, groups = first, []
    while low < lax.axis_size(axis):
        members = min(4, lax.axis_size(axis) // low)
        groups.append((low, members))
        low *= members
    return groups


def total_of(parts):
    return sum(part.astype(F32) for part in parts).astype(BF16)


def scattered_sum(values, axis, low, members, riders):
    digit = (lax.axis_index(axis) // low) % members

    def piece(value, k):
        rows = value.shape[0] // members
        return lax.dynamic_slice_in_dim(value, (digit ^ k) * rows, rows, 0)

    sums = [[piece(value, 0)] for value in values]
    arrived = {}
    for k in range(members - 1, 0, -1):
        sent = [piece(value, k) for value in values] + riders.get(k, [])
        received = swapped(jnp.concatenate(sent, axis=0), axis, k * low)
        start = 0
        for total in sums:
            total.append(received[start : start + total[0].shape[0]])
            start += total[0].shape[0]
        arrived[k] = received[start:]
    return [total_of(total) for total in sums], arrived


def exchanged(value, axis, low, members):
    return {k * low: swapped(value, axis, k * low) for k in range(members - 1, 0, -1)}


def shards(
    embed,
    cotangent,
    basis,
    triplet_row_index,
    triplet_slot_count,
    outgoing_edge_rows,
    residual_weight,
    down_weight,
    up_weight,
    basis_weight,
):
    rows, inner = embed.shape
    trips, nbasis = basis.shape[:2]

    *sends, embed_v, outgoing_v = select(embed, outgoing_edge_rows)
    ghosts = pair_exchange(sends)
    down_v, index_v, count_v, up_v, bw_v, dres, mine, other, pre, proj = residual(
        embed_v,
        residual_weight,
        cotangent,
        down_weight.T,
        triplet_row_index,
        triplet_slot_count.reshape(1, rows),
        up_weight,
        basis_weight,
    )
    share = total_of([mine, swapped(other, "brick", 1)])

    own, first, second, last, mine, other = triplets(
        proj,
        pre,
        embed_v,
        down_v,
        ghosts,
        basis.reshape(trips * nbasis, rows),
        index_v,
        count_v,
        up_v,
        cotangent,
        bw_v,
    )
    mine, other, share = lax.optimization_barrier((mine, other, share))
    received = swapped(other, "brick", 1)
    shared = mine.shape[0]
    mine = total_of([mine, received[:shared]])
    ring = lax.axis_size("slab")
    riders = {1: [first]}
    if ring == 4:
        riders[3] = [second]
    backs = [None, None, received[shared:], paired(last, "brick", 1)]
    slab_groups = groups_of("slab", 1)
    for low, members in reversed(slab_groups):
        (share, mine), arrived = scattered_sum(
            [share, mine], "slab", low, members, riders if low == 1 else {}
        )
    backs[0] = arrived[1]
    backs[1] = arrived[3] if ring == 4 else paired(second, "slab", 1)
    edge_grad = edge_gradient(own, backs, outgoing_v, pre, residual_weight, down_v, dres)

    value = jnp.concatenate([share, mine], axis=0)
    for low, members in groups_of("brick", 2):
        value = total_of([value, *exchanged(value, "brick", low, members).values()])
    value, edge_grad = lax.optimization_barrier((value, edge_grad))
    pieces = {0: value}
    for low, members in slab_groups:
        known = sorted(pieces)
        value = jnp.concatenate([pieces[o] for o in known], axis=0)
        for k, other in exchanged(value, "slab", low, members).items():
            for i, offset in enumerate(known):
                step = pieces[offset].shape[0]
                pieces[offset ^ k] = other[i * step : (i + 1) * step]
    value = jnp.concatenate([pieces[o] for o in sorted(pieces)], axis=0)
    residual_grad, down_grad, up_grad, basis_grad = finish(
        sorted(pieces), value, swapped(value, "brick", 1), shared, inner, proj.shape[0], nbasis
    )
    return edge_grad, residual_grad, down_grad.T, up_grad, basis_grad


def solution(mesh):
    both = P(AXES, None)
    in_specs = (both, both, P(None, None, AXES), P(None, AXES), P(AXES), P(None, AXES)) + (P(),) * 4
    out_specs = (both, P(), P(), P(), P())
    return jax.shard_map(shards, mesh=mesh, in_specs=in_specs, out_specs=out_specs, check_vma=False)
```

```python
import jax
import jax.numpy as jnp
from jax import lax
from jax.experimental import pallas as pl
from jax.experimental.pallas import tpu as pltpu
from jax.sharding import PartitionSpec as P

AXES = ("slab", "brick")
LANES = 256
F32 = jnp.float32
BF16 = jnp.bfloat16
NN = ((1,), (0,))
NT = ((1,), (1,))
TN = ((0,), (0,))
VMEM = pl.BlockSpec(memory_space=pltpu.VMEM)
HBM = pl.BlockSpec(memory_space=pltpu.HBM)


def dot(a, b, dims, precision=None):
    return lax.dot_general(a, b, (dims, ((), ())), precision=precision, preferred_element_type=F32)


def like(*arrays):
    return [jax.ShapeDtypeStruct(a.shape, a.dtype) for a in arrays]


def in_hbm(*arrays):
    return [pltpu.with_memory_space_constraint(a, pltpu.HBM) for a in arrays]


def limits():
    return pltpu.CompilerParams(vmem_limit_bytes=30 * 2**20)


def cost(flops):
    return pl.CostEstimate(flops=flops, bytes_accessed=0, transcendentals=0)


def in_vmem(*arrays):
    return [pltpu.VMEM(a.shape, a.dtype) for a in arrays]


def blocks_of(width):
    return [pl.ds(start, 128) for start in range(0, width, 128)]


def sigmoid(value):
    return 1.0 / (1.0 + jnp.exp(-value))


def silu_grad(value):
    sig = sigmoid(value)
    return sig * (1.0 + value * (1.0 - sig))


def parity(axis):
    return lax.axis_index(axis) % 2 == 1


def onehot(low):
    rows = lax.broadcasted_iota(jnp.int32, (LANES, low.shape[1]), 0).astype(jnp.int16)
    return jnp.where(rows == low.astype(jnp.int16), jnp.ones((), BF16), jnp.zeros((), BF16))


def stacked(table):
    return jnp.concatenate(
        [table[:, g * LANES : (g + 1) * LANES] for g in range(table.shape[1] // LANES)], axis=0
    )


def unstacked(blocks, width):
    return jnp.concatenate(
        [blocks[g * width : (g + 1) * width] for g in range(blocks.shape[0] // width)], axis=1
    )


def chosen(blocks, high, width):
    total = jnp.zeros((width, blocks.shape[1]), F32)
    for g in range(blocks.shape[0] // width):
        total = jnp.where(high == g, blocks[g * width : (g + 1) * width], total)
    return total


def spread(values, high, groups):
    zero = jnp.zeros_like(values)
    return jnp.concatenate([jnp.where(high == g, values, zero) for g in range(groups)], axis=0)


def pair_lists(rows_ref):
    lists = []
    for first, axis in ((0, "slab"), (2, "brick")):
        odd = parity(axis)
        up, down = rows_ref[first : first + 1, :], rows_ref[first + 1 : first + 2, :]
        lists += [jnp.where(odd, down, up), jnp.where(odd, up, down)]
    return lists


def paired(value, axis, first):
    count = lax.axis_size(axis)
    pairs = []
    for i in range(first, count, 2):
        j = (i + 1) % count
        pairs += [(i, j), (j, i)]
    return lax.ppermute(value, axis, pairs)


def pair_exchange(values):
    spots = (("slab", 0), ("slab", 1), ("brick", 0), ("brick", 1))
    sent = {k: paired(values[k], *spots[k]) for k in (3, 1, 0, 2)}
    return [sent[k] for k in range(4)]


def select_kernel(embed_ref, rows_ref, s0, s1, s2, s3, embed_v, rows_v, sems):
    copies = [
        pltpu.make_async_copy(rows_ref, rows_v, sems.at[0]),
        pltpu.make_async_copy(embed_ref, embed_v, sems.at[1]),
    ]
    for copy in copies:
        copy.start()
    for copy in copies:
        copy.wait()
    rows = embed_v.shape[0]
    for index, send_ref in zip(pair_lists(rows_v), (s0, s1, s2, s3)):
        spots = lax.broadcasted_iota(jnp.int32, (rows, index.shape[1]), 0).astype(jnp.int16)
        hot = jnp.where(spots == index.astype(jnp.int16), jnp.ones((), BF16), jnp.zeros((), BF16))
        send_ref[...] = dot(hot, embed_v[...], TN).astype(BF16)


def select(embed, outgoing):
    ghost = jax.ShapeDtypeStruct((outgoing.shape[1], embed.shape[1]), BF16)
    return pl.pallas_call(
        select_kernel,
        in_specs=[HBM] * 2,
        out_specs=[VMEM] * 6,
        out_shape=in_vmem(*[ghost] * 4, embed, outgoing),
        scratch_shapes=[pltpu.SemaphoreType.DMA((2,))],
        compiler_params=limits(),
        name="select",
    )(*in_hbm(embed, outgoing))


def residual_kernel(embed_ref, weight_ref, cotangent_ref, *refs):
    count = (len(refs) - 8) // 2
    sources, targets = refs[:count], refs[count : 2 * count]
    dres_ref, mine_ref, other_ref, pre_ref = refs[2 * count : 2 * count + 4]
    cotangent_v, dres_v, grad_ref, sems = refs[2 * count + 4 :]
    rows = embed_ref.shape[0]
    block = min(rows, LANES)
    spans = [pl.ds(start, block) for start in range(0, rows, block)]
    reads = [
        pltpu.make_async_copy(cotangent_ref.at[at, :], cotangent_v.at[at, :], sems.at[i])
        for i, at in enumerate(spans)
    ]
    writes = [
        pltpu.make_async_copy(dres_v.at[at, :], dres_ref.at[at, :], sems.at[len(spans) + i])
        for i, at in enumerate(spans)
    ]
    copies = [
        pltpu.make_async_copy(source, target, sems.at[2 * len(spans) + i])
        for i, (source, target) in enumerate(zip(sources, targets))
    ]
    for copy in reads + copies:
        copy.start()
    for at, read, write in zip(spans, reads, writes):
        res_pre = dot(embed_ref[at, :], weight_ref[...], NN)
        grad = silu_grad(res_pre)
        read.wait()
        dres_v[at, :] = (cotangent_v[at, :].astype(F32) * grad).astype(BF16)
        write.start()
    copies[0].wait()
    pre_ref[...] = dot(targets[0][...], embed_ref[...], NT)
    grad_ref[...] = dot(embed_ref[...], dres_v[...], TN).astype(BF16)
    half = grad_ref.shape[0] // 2
    upper = lax.axis_index("brick") % 2
    columns = blocks_of(grad_ref.shape[1])
    step = half // lax.axis_size("slab")
    for part in range(half // step):
        for c, column in enumerate(columns):
            to = pl.ds((part * len(columns) + c) * step, step)
            mine_ref[to, :] = grad_ref[pl.ds(upper * half + part * step, step), column]
            other_ref[to, :] = grad_ref[pl.ds((1 - upper) * half + part * step, step), column]
    for copy in writes + copies[1:]:
        copy.wait()


def residual(embed, weight, cotangent, down_t, *staged):
    staged = (down_t, *staged)
    width, rows = down_t.shape[0], embed.shape[0]
    half = jax.ShapeDtypeStruct((weight.size // 256, 128), BF16)
    blocks = embed.shape[0] // min(embed.shape[0], LANES)
    return pl.pallas_call(
        residual_kernel,
        in_specs=[VMEM] * 2 + [HBM] * (1 + len(staged)),
        out_specs=[VMEM] * len(staged) + [HBM] + [VMEM] * 3,
        out_shape=in_vmem(*staged)
        + [pltpu.HBM(embed.shape, BF16)]
        + in_vmem(half, half)
        + [pltpu.VMEM((width, rows), F32)],
        scratch_shapes=[
            pltpu.VMEM(embed.shape, BF16),
            pltpu.VMEM(embed.shape, BF16),
            pltpu.VMEM(weight.shape, BF16),
            pltpu.SemaphoreType.DMA((2 * blocks + len(staged),)),
        ],
        compiler_params=limits(),
        cost_estimate=cost(6 * embed.size * weight.shape[1]),
        name="residual",
    )(embed, weight, *in_hbm(cotangent, *staged))


def triplet_kernel(
    pre_ref,
    embed_ref,
    down_ref,
    g0_ref,
    g1_ref,
    g2_ref,
    g3_ref,
    index_ref,
    count_ref,
    bw_ref,
    basis_hbm,
    cotangent_hbm,
    up_hbm,
    own_ref,
    t0_ref,
    t1_ref,
    t3_ref,
    mine_ref,
    other_ref,
    ghost_embed_ref,
    rest_ref,
    table_ref,
    weight_ref,
    hot_ref,
    picked_ref,
    dw_ref,
    tsum_ref,
    dt_ref,
    acc_ref,
    basis_ref,
    cotangent_ref,
    up_ref,
    sems,
):
    read_basis = pltpu.make_async_copy(basis_hbm, basis_ref, sems.at[0])
    read_cotangent = pltpu.make_async_copy(cotangent_hbm, cotangent_ref, sems.at[1])
    read_up = pltpu.make_async_copy(up_hbm, up_ref, sems.at[2])
    read_basis.start()
    read_cotangent.start()
    read_up.start()
    width, rows = pre_ref.shape
    trips = index_ref.shape[0]
    nbasis = bw_ref.shape[0]
    own_groups = rows // LANES
    ghost = g0_ref.shape[0]
    for first, a_ref, b_ref, axis in ((0, g0_ref, g1_ref, "slab"), (2, g2_ref, g3_ref, "brick")):
        odd = parity(axis)
        a, b = a_ref[...], b_ref[...]
        ghost_embed_ref[first * ghost : (first + 1) * ghost, :] = jnp.where(odd, a, b)
        ghost_embed_ref[(first + 1) * ghost : (first + 2) * ghost, :] = jnp.where(odd, b, a)
    ghost_pre = dot(down_ref[...], ghost_embed_ref[...], NT)
    ghost_grad = silu_grad(ghost_pre)
    own_pre = pre_ref[...]
    table_ref[: own_groups * width, :] = stacked((own_pre * sigmoid(own_pre)).astype(BF16))
    table_ref[own_groups * width :, :] = stacked((ghost_pre * sigmoid(ghost_pre)).astype(BF16))
    groups = table_ref.shape[0] // width
    tiles = rows // LANES

    span = trips * nbasis
    fold = jnp.where(
        lax.broadcasted_iota(jnp.int32, (nbasis, span), 1) % nbasis
        == lax.broadcasted_iota(jnp.int32, (nbasis, span), 0),
        1.0,
        0.0,
    )
    wide = dot(bw_ref[...], fold.astype(BF16), TN).astype(BF16)
    own_slot = lax.broadcasted_iota(jnp.int32, (trips, width, span), 0) == (
        lax.broadcasted_iota(jnp.int32, (trips, width, span), 2) // nbasis
    )
    diagonal = jnp.where(own_slot, wide[None], jnp.zeros((), BF16)).reshape(trips * width, span)
    read_basis.wait()
    weight_ref[...] = dot(diagonal, basis_ref[...], NN)

    tsum_ref[...] = jnp.zeros_like(tsum_ref)

    def lookup(j, t):
        at = pl.ds(t * LANES, LANES)
        index = index_ref[pl.ds(j, 1), at]
        high = jnp.where(j < count_ref[:, at], index // LANES, -1)
        return at, index & (LANES - 1), high

    def forward(j, carry):
        for t in range(tiles):
            at, low, high = lookup(j, t)
            hot = onehot(low)
            hot_ref[j, :, at] = hot
            picked = chosen(dot(table_ref[...], hot, NN), high, width)
            picked_ref[j, :, at] = picked.astype(BF16)
            tsum_ref[:, at] += weight_ref[pl.ds(j * width, width), at] * picked
        return carry

    lax.fori_loop(0, trips, forward, 0, unroll=8)

    tsum = tsum_ref[...]
    sig = sigmoid(tsum)
    act = (tsum * sig).astype(BF16)
    read_cotangent.wait()
    read_up.wait()
    cotangent = cotangent_ref[...]
    inner = cotangent.shape[1]
    rest_ref[:, inner : 2 * inner] = dot(act, cotangent, NN).astype(BF16)
    dsum = dot(up_ref[...], cotangent, NT)
    dt_ref[...] = dsum * (sig * (1.0 + tsum * (1.0 - sig)))
    acc_ref[...] = jnp.zeros_like(acc_ref)

    def backward(j, carry):
        parts = []
        for t in range(tiles):
            at, low, high = lookup(j, t)
            dt = dt_ref[:, at]
            dw_ref[pl.ds(j * width, width), at] = (dt * picked_ref[j, :, at].astype(F32)).astype(BF16)
            terms = (dt * weight_ref[pl.ds(j * width, width), at]).astype(BF16)
            parts.append(spread(terms, high, groups))
        acc_ref[...] += dot(jnp.concatenate(parts, axis=1), hot_ref[j], NT)
        return carry

    lax.fori_loop(0, trips, backward, 0, unroll=8)

    own = unstacked(acc_ref[: own_groups * width, :], width)
    own_ref[...] = own
    ghost_terms = unstacked(acc_ref[own_groups * width :, :], width)
    sides = []
    for first, axis in ((0, "slab"), (2, "brick")):
        odd = parity(axis)
        prev = ghost_terms[:, first * ghost : (first + 1) * ghost].astype(BF16)
        following = ghost_terms[:, (first + 1) * ghost : (first + 2) * ghost].astype(BF16)
        sides += [jnp.where(odd, prev, following), jnp.where(odd, following, prev)]
    t0_ref[...], t1_ref[...], t3_ref[...] = sides[0], sides[1], sides[3]
    down_grad = dot((own * silu_grad(pre_ref[...])).astype(BF16), embed_ref[...], NN)
    down_grad += dot((ghost_terms * ghost_grad).astype(BF16), ghost_embed_ref[...], NN)
    rest_ref[:, :inner] = down_grad.astype(BF16)
    full = dot(dw_ref[...], basis_ref[...], NT).reshape(trips, width, span)
    kept = jnp.sum(jnp.where(own_slot, full, 0.0), axis=0)
    folded = dot(kept, fold, NT, lax.Precision.HIGHEST)
    pad = rest_ref.shape[1] - 2 * inner - nbasis
    rest_ref[:, 2 * inner :] = jnp.concatenate(
        [folded, jnp.zeros((width, pad), F32)], axis=1
    ).astype(BF16)
    half = width // 2
    upper = lax.axis_index("brick") % 2
    columns = blocks_of(rest_ref.shape[1])
    for c, column in enumerate(columns):
        to = pl.ds(c * half, half)
        mine_ref[to, :] = rest_ref[pl.ds(upper * half, half), column]
        other_ref[to, :] = rest_ref[pl.ds((1 - upper) * half, half), column]
    used, total = len(columns) * half, mine_ref.shape[0]
    if used < total:
        mine_ref[used:, :] = jnp.zeros((total - used, 128), BF16)
        other_ref[used:total, :] = jnp.zeros((total - used, 128), BF16)
    for c, column in enumerate(blocks_of(ghost)):
        other_ref[pl.ds(total + c * width, width), :] = sides[2][:, column]


def triplets(
    pre, embed, down_t, ghosts, basis, index, count, up_weight, cotangent, basis_weight
):
    width, rows = pre.shape
    trips = index.shape[0]
    ghost, inner = ghosts[0].shape
    groups = (rows + 4 * ghost) // LANES
    operands = (pre, embed, down_t, *ghosts, index, count, basis_weight)
    unit = 16 * lax.axis_size("slab")
    total = 2 * inner + 128
    shared = -(-(width * total // 256) // unit) * unit
    out_shape = (
        [pltpu.VMEM((width, rows), F32)]
        + [pltpu.VMEM((width, ghost), BF16)] * 3
        + [pltpu.VMEM((shared, 128), BF16), pltpu.VMEM((shared + width * ghost // 128, 128), BF16)]
    )
    return pl.pallas_call(
        triplet_kernel,
        in_specs=[VMEM] * len(operands) + [HBM] * 3,
        out_specs=[VMEM] * len(out_shape),
        out_shape=out_shape,
        scratch_shapes=[
            pltpu.VMEM((4 * ghost, inner), BF16),
            pltpu.VMEM((width, total), BF16),
            pltpu.VMEM((groups * width, LANES), BF16),
            pltpu.VMEM((trips * width, rows), F32),
            pltpu.VMEM((trips, LANES, rows), BF16),
            pltpu.VMEM((trips, width, rows), BF16),
            pltpu.VMEM((trips * width, rows), BF16),
            pltpu.VMEM((width, rows), F32),
            pltpu.VMEM((width, rows), F32),
            pltpu.VMEM((groups * width, LANES), F32),
            pltpu.VMEM(basis.shape, BF16),
            pltpu.VMEM(cotangent.shape, BF16),
            pltpu.VMEM(up_weight.shape, BF16),
            pltpu.SemaphoreType.DMA((3,)),
        ],
        compiler_params=limits(),
        cost_estimate=cost(8 * trips * rows * width * (rows + 4 * ghost)),
        name="triplets",
    )(*operands, *in_hbm(basis, cotangent, up_weight))


def edge_kernel(
    own_ref,
    b0_ref,
    b1_ref,
    b2_ref,
    b3_ref,
    rows_ref,
    pre_ref,
    weight_ref,
    down_ref,
    dres_hbm,
    out_ref,
    dres_ref,
    sems,
):
    width, rows = own_ref.shape
    block = min(rows, LANES)
    spans = [pl.ds(start, block) for start in range(0, rows, block)]
    reads = [
        pltpu.make_async_copy(dres_hbm.at[at, :], dres_ref.at[at, :], sems.at[i])
        for i, at in enumerate(spans)
    ]
    for read in reads:
        read.start()
    groups = rows // LANES
    acc = jnp.zeros((groups * width, LANES), F32)
    for index, back_ref in zip(pair_lists(rows_ref), (b0_ref, b1_ref, b2_ref, b3_ref)):
        acc += dot(spread(back_ref[...], index // LANES, groups), onehot(index & (LANES - 1)), NT)
    dproj = own_ref[...] + unstacked(acc, width)
    dpre = (dproj * silu_grad(pre_ref[...])).astype(BF16)
    for i, (at, read) in enumerate(zip(spans, reads)):
        down_term = dot(dpre[:, i * block : (i + 1) * block], down_ref[...], TN)
        read.wait()
        out_ref[at, :] = (dot(dres_ref[at, :], weight_ref[...], NT) + down_term).astype(BF16)


def edge_gradient(own, backs, outgoing, pre, weight, down_t, dres):
    rows, inner = dres.shape
    operands = (own, *backs, outgoing, pre, weight, down_t)
    return pl.pallas_call(
        edge_kernel,
        in_specs=[VMEM] * len(operands) + [HBM],
        out_specs=VMEM,
        out_shape=jax.ShapeDtypeStruct((rows, inner), BF16),
        scratch_shapes=[
            pltpu.VMEM((rows, inner), BF16),
            pltpu.SemaphoreType.DMA((rows // min(rows, LANES),)),
        ],
        compiler_params=limits(),
        cost_estimate=cost(4 * rows * inner * (inner + down_t.shape[0])),
        name="edge_gradient",
    )(*operands, *in_hbm(dres))


def finish_kernel(
    offsets, mine_ref, other_ref, residual_ref, down_ref, up_ref, basis_ref, all_ref, part_ref
):
    upper = lax.axis_index("brick") % 2
    slab = lax.axis_index("slab")
    half = residual_ref.shape[0] // 2
    step = half // len(offsets)
    columns = blocks_of(residual_ref.shape[1])
    block = mine_ref.shape[0] // len(offsets)
    tail = len(columns) * step
    share = block - tail
    for source, side in ((mine_ref, upper), (other_ref, 1 - upper)):
        for i, offset in enumerate(offsets):
            place = pl.ds(side * half + (slab ^ offset) * step, step)
            for c, column in enumerate(columns):
                at = pl.ds(i * block + c * step, step)
                residual_ref[place, column] = source[at, :].astype(F32)
            place = pl.ds((side * len(offsets) + (slab ^ offset)) * share, share)
            part_ref[place, :] = source[pl.ds(i * block + tail, share), :].astype(F32)
    rows, inner = all_ref.shape[0] // 2, down_ref.shape[1]
    for side in range(2):
        for c, column in enumerate(blocks_of(all_ref.shape[1])):
            at = pl.ds(side * len(offsets) * share + c * rows, rows)
            all_ref[pl.ds(side * rows, rows), column] = part_ref[at, :]
    down_ref[...] = all_ref[:, :inner]
    up_ref[...] = all_ref[:, inner : 2 * inner]
    basis_ref[...] = all_ref[:, 2 * inner :].T[: basis_ref.shape[0], :]


def finish(offsets, mine, other, shared, inner, width, nbasis):
    return pl.pallas_call(
        lambda *refs: finish_kernel(offsets, *refs),
        in_specs=[VMEM] * 2,
        out_specs=[VMEM] * 4,
        out_shape=[
            jax.ShapeDtypeStruct((inner, inner), F32),
            jax.ShapeDtypeStruct((width, inner), F32),
            jax.ShapeDtypeStruct((width, inner), F32),
            jax.ShapeDtypeStruct((nbasis, width), F32),
        ],
        scratch_shapes=[
            pltpu.VMEM((width, 2 * inner + 128), F32),
            pltpu.VMEM((2 * shared, 128), F32),
        ],
        compiler_params=limits(),
        name="finish",
    )(mine, other)


def swapped(value, axis, offset):
    return lax.ppermute(value, axis, [(i, i ^ offset) for i in range(lax.axis_size(axis))])


def groups_of(axis, first):
    low, groups = first, []
    while low < lax.axis_size(axis):
        members = min(4, lax.axis_size(axis) // low)
        groups.append((low, members))
        low *= members
    return groups


def total_of(parts):
    return sum(part.astype(F32) for part in parts).astype(BF16)


def scattered_sum(values, axis, low, members, riders):
    digit = (lax.axis_index(axis) // low) % members

    def piece(value, k):
        rows = value.shape[0] // members
        return lax.dynamic_slice_in_dim(value, (digit ^ k) * rows, rows, 0)

    sums = [[piece(value, 0)] for value in values]
    arrived = {}
    for k in range(members - 1, 0, -1):
        sent = [piece(value, k) for value in values] + riders.get(k, [])
        received = swapped(jnp.concatenate(sent, axis=0), axis, k * low)
        start = 0
        for total in sums:
            total.append(received[start : start + total[0].shape[0]])
            start += total[0].shape[0]
        arrived[k] = received[start:]
    return [total_of(total) for total in sums], arrived


def exchanged(value, axis, low, members):
    return {k * low: swapped(value, axis, k * low) for k in range(members - 1, 0, -1)}


def shards(
    embed,
    cotangent,
    basis,
    triplet_row_index,
    triplet_slot_count,
    outgoing_edge_rows,
    residual_weight,
    down_weight,
    up_weight,
    basis_weight,
):
    rows, inner = embed.shape
    trips, nbasis = basis.shape[:2]

    *sends, embed_v, outgoing_v = select(embed, outgoing_edge_rows)
    ghosts = pair_exchange(sends)
    down_v, index_v, count_v, bw_v, dres, mine, other, pre = residual(
        embed_v,
        residual_weight,
        cotangent,
        down_weight.T,
        triplet_row_index,
        triplet_slot_count.reshape(1, rows),
        basis_weight,
    )
    share = total_of([mine, swapped(other, "brick", 1)])

    own, first, second, last, mine, other = triplets(
        pre,
        embed_v,
        down_v,
        ghosts,
        basis.reshape(trips * nbasis, rows),
        index_v,
        count_v,
        up_weight,
        cotangent,
        bw_v,
    )
    received = swapped(other, "brick", 1)
    shared = mine.shape[0]
    mine = total_of([mine, received[:shared]])
    ring = lax.axis_size("slab")
    riders = {1: [first]}
    if ring == 4:
        riders[3] = [second]
    backs = [None, None, received[shared:], paired(last, "brick", 1)]
    slab_groups = groups_of("slab", 1)
    for low, members in reversed(slab_groups):
        (share, mine), arrived = scattered_sum(
            [share, mine], "slab", low, members, riders if low == 1 else {}
        )
    backs[0] = arrived[1]
    backs[1] = arrived[3] if ring == 4 else paired(second, "slab", 1)
    edge_grad = edge_gradient(own, backs, outgoing_v, pre, residual_weight, down_v, dres)

    value = jnp.concatenate([share, mine], axis=0)
    for low, members in groups_of("brick", 2):
        value = total_of([value, *exchanged(value, "brick", low, members).values()])
    value, edge_grad = lax.optimization_barrier((value, edge_grad))
    pieces = {0: value}
    for low, members in slab_groups:
        known = sorted(pieces)
        value = jnp.concatenate([pieces[o] for o in known], axis=0)
        for k, other in exchanged(value, "slab", low, members).items():
            for i, offset in enumerate(known):
                step = pieces[offset].shape[0]
                pieces[offset ^ k] = other[i * step : (i + 1) * step]
    value = jnp.concatenate([pieces[o] for o in sorted(pieces)], axis=0)
    residual_grad, down_grad, up_grad, basis_grad = finish(
        sorted(pieces), value, swapped(value, "brick", 1), shared, inner, pre.shape[0], nbasis
    )
    return edge_grad, residual_grad, down_grad.T, up_grad, basis_grad


def solution(mesh):
    both = P(AXES, None)
    in_specs = (both, both, P(None, None, AXES), P(None, AXES), P(AXES), P(None, AXES)) + (P(),) * 4
    out_specs = (both, P(), P(), P(), P())
    return jax.shard_map(shards, mesh=mesh, in_specs=in_specs, out_specs=out_specs, check_vma=False)
```

```python
import jax
import jax.numpy as jnp
from jax import lax
from jax.experimental import pallas as pl
from jax.experimental.pallas import tpu as pltpu
from jax.sharding import PartitionSpec as P

AXES = ("slab", "brick")
LANES = 256
F32 = jnp.float32
BF16 = jnp.bfloat16
NN = ((1,), (0,))
NT = ((1,), (1,))
TN = ((0,), (0,))
VMEM = pl.BlockSpec(memory_space=pltpu.VMEM)
HBM = pl.BlockSpec(memory_space=pltpu.HBM)


def dot(a, b, dims, precision=None):
    return lax.dot_general(a, b, (dims, ((), ())), precision=precision, preferred_element_type=F32)


def like(*arrays):
    return [jax.ShapeDtypeStruct(a.shape, a.dtype) for a in arrays]


def in_hbm(*arrays):
    return [pltpu.with_memory_space_constraint(a, pltpu.HBM) for a in arrays]


def limits():
    return pltpu.CompilerParams(vmem_limit_bytes=30 * 2**20)


def cost(flops):
    return pl.CostEstimate(flops=flops, bytes_accessed=0, transcendentals=0)


def in_vmem(*arrays):
    return [pltpu.VMEM(a.shape, a.dtype) for a in arrays]


def blocks_of(width):
    return [pl.ds(start, 128) for start in range(0, width, 128)]


def sigmoid(value):
    return 1.0 / (1.0 + jnp.exp(-value))


def silu_grad(value):
    sig = sigmoid(value)
    return sig * (1.0 + value * (1.0 - sig))


def parity(axis):
    return lax.axis_index(axis) % 2 == 1


def onehot(low):
    rows = lax.broadcasted_iota(jnp.int32, (LANES, low.shape[1]), 0).astype(jnp.int16)
    return jnp.where(rows == low.astype(jnp.int16), jnp.ones((), BF16), jnp.zeros((), BF16))


def stacked(table):
    return jnp.concatenate(
        [table[:, g * LANES : (g + 1) * LANES] for g in range(table.shape[1] // LANES)], axis=0
    )


def unstacked(blocks, width):
    return jnp.concatenate(
        [blocks[g * width : (g + 1) * width] for g in range(blocks.shape[0] // width)], axis=1
    )


def chosen(blocks, high, width):
    total = jnp.zeros((width, blocks.shape[1]), F32)
    for g in range(blocks.shape[0] // width):
        total = jnp.where(high == g, blocks[g * width : (g + 1) * width], total)
    return total


def spread(values, high, groups):
    zero = jnp.zeros_like(values)
    return jnp.concatenate([jnp.where(high == g, values, zero) for g in range(groups)], axis=0)


def pair_lists(rows_ref):
    lists = []
    for first, axis in ((0, "slab"), (2, "brick")):
        odd = parity(axis)
        up, down = rows_ref[first : first + 1, :], rows_ref[first + 1 : first + 2, :]
        lists += [jnp.where(odd, down, up), jnp.where(odd, up, down)]
    return lists


def paired(value, axis, first):
    count = lax.axis_size(axis)
    pairs = []
    for i in range(first, count, 2):
        j = (i + 1) % count
        pairs += [(i, j), (j, i)]
    return lax.ppermute(value, axis, pairs)


def pair_exchange(values):
    spots = (("slab", 0), ("slab", 1), ("brick", 0), ("brick", 1))
    sent = {k: paired(values[k], *spots[k]) for k in (3, 1, 0, 2)}
    return [sent[k] for k in range(4)]


def select_kernel(
    embed_ref, rows_ref, weight_ref, s0, s1, s2, s3, embed_v, rows_v, weight_v, sems
):
    copies = [
        pltpu.make_async_copy(rows_ref, rows_v, sems.at[0]),
        pltpu.make_async_copy(embed_ref, embed_v, sems.at[1]),
        pltpu.make_async_copy(weight_ref, weight_v, sems.at[2]),
    ]
    for copy in copies:
        copy.start()
    for copy in copies[:2]:
        copy.wait()
    rows = embed_v.shape[0]
    for index, send_ref in zip(pair_lists(rows_v), (s0, s1, s2, s3)):
        spots = lax.broadcasted_iota(jnp.int32, (rows, index.shape[1]), 0).astype(jnp.int16)
        hot = jnp.where(spots == index.astype(jnp.int16), jnp.ones((), BF16), jnp.zeros((), BF16))
        send_ref[...] = dot(hot, embed_v[...], TN).astype(BF16)
    copies[2].wait()


def select(embed, outgoing, weight):
    ghost = jax.ShapeDtypeStruct((outgoing.shape[1], embed.shape[1]), BF16)
    return pl.pallas_call(
        select_kernel,
        in_specs=[HBM] * 3,
        out_specs=[VMEM] * 7,
        out_shape=in_vmem(*[ghost] * 4, embed, outgoing, weight),
        scratch_shapes=[pltpu.SemaphoreType.DMA((3,))],
        compiler_params=limits(),
        name="select",
    )(*in_hbm(embed, outgoing, weight))


def residual_kernel(embed_ref, weight_ref, cotangent_ref, basis_hbm, bw_hbm, *refs):
    count = (len(refs) - 11) // 2
    sources, targets = refs[:count], refs[count : 2 * count]
    dres_ref, mine_ref, other_ref, pre_ref, slots_ref = refs[2 * count : 2 * count + 5]
    cotangent_v, dres_v, grad_ref, basis_ref, bw_ref, sems = refs[2 * count + 5 :]
    rows = embed_ref.shape[0]
    block = min(rows, LANES)
    spans = [pl.ds(start, block) for start in range(0, rows, block)]
    reads = [
        pltpu.make_async_copy(cotangent_ref.at[at, :], cotangent_v.at[at, :], sems.at[i])
        for i, at in enumerate(spans)
    ]
    writes = [
        pltpu.make_async_copy(dres_v.at[at, :], dres_ref.at[at, :], sems.at[len(spans) + i])
        for i, at in enumerate(spans)
    ]
    copies = [
        pltpu.make_async_copy(source, target, sems.at[2 * len(spans) + i])
        for i, (source, target) in enumerate(
            zip((*sources, basis_hbm, bw_hbm), (*targets, basis_ref, bw_ref))
        )
    ]
    for copy in reads + copies:
        copy.start()
    for at, read, write in zip(spans, reads, writes):
        res_pre = dot(embed_ref[at, :], weight_ref[...], NN)
        grad = silu_grad(res_pre)
        read.wait()
        dres_v[at, :] = (cotangent_v[at, :].astype(F32) * grad).astype(BF16)
        write.start()
    copies[0].wait()
    pre_ref[...] = dot(targets[0][...], embed_ref[...], NT)
    grad_ref[...] = dot(embed_ref[...], dres_v[...], TN).astype(BF16)
    half = grad_ref.shape[0] // 2
    upper = lax.axis_index("brick") % 2
    columns = blocks_of(grad_ref.shape[1])
    step = half // lax.axis_size("slab")
    for part in range(half // step):
        for c, column in enumerate(columns):
            to = pl.ds((part * len(columns) + c) * step, step)
            mine_ref[to, :] = grad_ref[pl.ds(upper * half + part * step, step), column]
            other_ref[to, :] = grad_ref[pl.ds((1 - upper) * half + part * step, step), column]
    for copy in copies[1:]:
        copy.wait()
    nbasis, width = bw_ref.shape
    span = basis_ref.shape[0]
    trips = span // nbasis
    fold = jnp.where(
        lax.broadcasted_iota(jnp.int32, (nbasis, span), 1) % nbasis
        == lax.broadcasted_iota(jnp.int32, (nbasis, span), 0),
        1.0,
        0.0,
    )
    wide = dot(bw_ref[...], fold.astype(BF16), TN).astype(BF16)
    own_slot = lax.broadcasted_iota(jnp.int32, (trips, width, span), 0) == (
        lax.broadcasted_iota(jnp.int32, (trips, width, span), 2) // nbasis
    )
    diagonal = jnp.where(own_slot, wide[None], jnp.zeros((), BF16)).reshape(trips * width, span)
    slots_ref[...] = dot(diagonal, basis_ref[...], NN)

    for copy in writes:
        copy.wait()


def residual(embed, weight, cotangent, basis, basis_weight, down_t, *staged):
    staged = (down_t, *staged)
    width, rows = down_t.shape[0], embed.shape[0]
    trips = basis.shape[0] // basis_weight.shape[0]
    half = jax.ShapeDtypeStruct((weight.size // 256, 128), BF16)
    blocks = embed.shape[0] // min(embed.shape[0], LANES)
    return pl.pallas_call(
        residual_kernel,
        in_specs=[VMEM] * 2 + [HBM] * (3 + len(staged)),
        out_specs=[VMEM] * len(staged) + [HBM] + [VMEM] * 4,
        out_shape=in_vmem(*staged)
        + [pltpu.HBM(embed.shape, BF16)]
        + in_vmem(half, half)
        + [pltpu.VMEM((width, rows), F32), pltpu.VMEM((trips * width, rows), F32)],
        scratch_shapes=[
            pltpu.VMEM(embed.shape, BF16),
            pltpu.VMEM(embed.shape, BF16),
            pltpu.VMEM(weight.shape, BF16),
            pltpu.VMEM(basis.shape, BF16),
            pltpu.VMEM(basis_weight.shape, BF16),
            pltpu.SemaphoreType.DMA((2 * blocks + len(staged) + 2,)),
        ],
        compiler_params=limits(),
        cost_estimate=cost(6 * embed.size * weight.shape[1]),
        name="residual",
    )(embed, weight, *in_hbm(cotangent, basis, basis_weight, *staged))


def triplet_kernel(
    pre_ref,
    embed_ref,
    down_ref,
    g1_ref,
    g3_ref,
    g0_ref,
    g2_ref,
    index_ref,
    count_ref,
    weight_ref,
    basis_hbm,
    cotangent_hbm,
    up_hbm,
    own_ref,
    t0_ref,
    t1_ref,
    t3_ref,
    mine_ref,
    other_ref,
    ghost_embed_ref,
    rest_ref,
    table_ref,
    hot_ref,
    picked_ref,
    tsum_ref,
    dt_ref,
    acc_ref,
    basis_ref,
    cotangent_ref,
    up_ref,
    sems,
):
    read_basis = pltpu.make_async_copy(basis_hbm, basis_ref, sems.at[0])
    read_cotangent = pltpu.make_async_copy(cotangent_hbm, cotangent_ref, sems.at[1])
    read_up = pltpu.make_async_copy(up_hbm, up_ref, sems.at[2])
    read_basis.start()
    read_cotangent.start()
    read_up.start()
    width, rows = pre_ref.shape
    trips = index_ref.shape[0]
    nbasis = basis_ref.shape[0] // trips
    own_groups = rows // LANES
    ghost = g0_ref.shape[0]
    for first, a_ref, b_ref, axis in ((0, g0_ref, g1_ref, "slab"), (2, g2_ref, g3_ref, "brick")):
        odd = parity(axis)
        a, b = a_ref[...], b_ref[...]
        ghost_embed_ref[first * ghost : (first + 1) * ghost, :] = jnp.where(odd, a, b)
        ghost_embed_ref[(first + 1) * ghost : (first + 2) * ghost, :] = jnp.where(odd, b, a)
    ghost_pre = dot(down_ref[...], ghost_embed_ref[...], NT)
    ghost_grad = silu_grad(ghost_pre)
    own_pre = pre_ref[...]
    table_ref[: own_groups * width, :] = stacked((own_pre * sigmoid(own_pre)).astype(BF16))
    table_ref[own_groups * width :, :] = stacked((ghost_pre * sigmoid(ghost_pre)).astype(BF16))
    groups = table_ref.shape[0] // width
    tiles = rows // LANES

    tsum_ref[...] = jnp.zeros_like(tsum_ref)

    def lookup(j, t):
        at = pl.ds(t * LANES, LANES)
        index = index_ref[pl.ds(j, 1), at]
        high = jnp.where(j < count_ref[:, at], index // LANES, -1)
        return at, index & (LANES - 1), high

    def forward(j, carry):
        for t in range(tiles):
            at, low, high = lookup(j, t)
            hot = onehot(low)
            hot_ref[j, :, at] = hot
            picked = chosen(dot(table_ref[...], hot, NN), high, width)
            picked_ref[j, :, at] = picked.astype(BF16)
            tsum_ref[:, at] += weight_ref[pl.ds(j * width, width), at] * picked
        return carry

    lax.fori_loop(0, trips, forward, 0, unroll=16)

    tsum = tsum_ref[...]
    sig = sigmoid(tsum)
    act = (tsum * sig).astype(BF16)
    read_basis.wait()
    read_cotangent.wait()
    read_up.wait()
    cotangent = cotangent_ref[...]
    inner = cotangent.shape[1]
    rest_ref[:, inner : 2 * inner] = dot(act, cotangent, NN).astype(BF16)
    dsum = dot(up_ref[...], cotangent, NT)
    dt_ref[...] = dsum * (sig * (1.0 + tsum * (1.0 - sig)))
    acc_ref[...] = jnp.zeros_like(acc_ref)

    def backward(j, carry):
        parts = []
        dws = []
        for t in range(tiles):
            at, low, high = lookup(j, t)
            dt = dt_ref[:, at]
            dws.append((dt * picked_ref[j, :, at].astype(F32)).astype(BF16))
            terms = (dt * weight_ref[pl.ds(j * width, width), at]).astype(BF16)
            parts.append(spread(terms, high, groups))
        acc_ref[...] += dot(jnp.concatenate(parts, axis=1), hot_ref[j], NT)
        slot_basis = basis_ref[pl.ds(pl.multiple_of(j * nbasis, nbasis), nbasis), :]
        return carry + dot(slot_basis, jnp.concatenate(dws, axis=1), NT)

    basis_grad = lax.fori_loop(0, trips, backward, jnp.zeros((nbasis, width), F32), unroll=8)

    own = unstacked(acc_ref[: own_groups * width, :], width)
    own_ref[...] = own
    ghost_terms = unstacked(acc_ref[own_groups * width :, :], width)
    sides = []
    for first, axis in ((0, "slab"), (2, "brick")):
        odd = parity(axis)
        prev = ghost_terms[:, first * ghost : (first + 1) * ghost].astype(BF16)
        following = ghost_terms[:, (first + 1) * ghost : (first + 2) * ghost].astype(BF16)
        sides += [jnp.where(odd, prev, following), jnp.where(odd, following, prev)]
    t0_ref[...], t1_ref[...], t3_ref[...] = sides[0], sides[1], sides[3]
    down_grad = dot((own * silu_grad(pre_ref[...])).astype(BF16), embed_ref[...], NN)
    down_grad += dot((ghost_terms * ghost_grad).astype(BF16), ghost_embed_ref[...], NN)
    rest_ref[:, :inner] = down_grad.astype(BF16)
    rest_ref[:, 2 * inner :] = jnp.zeros((width, rest_ref.shape[1] - 2 * inner), BF16)
    rest_ref[:nbasis, 2 * inner : 2 * inner + width] = basis_grad.astype(BF16)
    half = width // 2
    upper = lax.axis_index("brick") % 2
    columns = blocks_of(rest_ref.shape[1])
    for c, column in enumerate(columns):
        to = pl.ds(c * half, half)
        mine_ref[to, :] = rest_ref[pl.ds(upper * half, half), column]
        other_ref[to, :] = rest_ref[pl.ds((1 - upper) * half, half), column]
    used, total = len(columns) * half, mine_ref.shape[0]
    if used < total:
        mine_ref[used:, :] = jnp.zeros((total - used, 128), BF16)
        other_ref[used:total, :] = jnp.zeros((total - used, 128), BF16)
    for c, column in enumerate(blocks_of(ghost)):
        other_ref[pl.ds(total + c * width, width), :] = sides[2][:, column]


def triplets(
    pre, embed, down_t, ghosts, basis, index, count, up_weight, cotangent, weights
):
    width, rows = pre.shape
    trips = index.shape[0]
    ghost, inner = ghosts[0].shape
    groups = (rows + 4 * ghost) // LANES
    ordered = [ghosts[k] for k in (1, 3, 0, 2)]
    operands = (pre, embed, down_t, *ordered, index, count, weights)
    unit = 16 * lax.axis_size("slab")
    total = 2 * inner + 128
    shared = -(-(width * total // 256) // unit) * unit
    out_shape = (
        [pltpu.VMEM((width, rows), F32)]
        + [pltpu.VMEM((width, ghost), BF16)] * 3
        + [pltpu.VMEM((shared, 128), BF16), pltpu.VMEM((shared + width * ghost // 128, 128), BF16)]
    )
    return pl.pallas_call(
        triplet_kernel,
        in_specs=[VMEM] * len(operands) + [HBM] * 3,
        out_specs=[VMEM] * len(out_shape),
        out_shape=out_shape,
        scratch_shapes=[
            pltpu.VMEM((4 * ghost, inner), BF16),
            pltpu.VMEM((width, total), BF16),
            pltpu.VMEM((groups * width, LANES), BF16),
            pltpu.VMEM((trips, LANES, rows), BF16),
            pltpu.VMEM((trips, width, rows), BF16),
            pltpu.VMEM((width, rows), F32),
            pltpu.VMEM((width, rows), F32),
            pltpu.VMEM((groups * width, LANES), F32),
            pltpu.VMEM(basis.shape, BF16),
            pltpu.VMEM(cotangent.shape, BF16),
            pltpu.VMEM(up_weight.shape, BF16),
            pltpu.SemaphoreType.DMA((3,)),
        ],
        compiler_params=limits(),
        cost_estimate=cost(8 * trips * rows * width * (rows + 4 * ghost)),
        name="triplets",
    )(*operands, *in_hbm(basis, cotangent, up_weight))


def edge_kernel(
    own_ref,
    b0_ref,
    b1_ref,
    b2_ref,
    b3_ref,
    rows_ref,
    pre_ref,
    weight_ref,
    down_ref,
    dres_hbm,
    out_ref,
    dres_ref,
    sems,
):
    width, rows = own_ref.shape
    block = min(rows, LANES)
    spans = [pl.ds(start, block) for start in range(0, rows, block)]
    reads = [
        pltpu.make_async_copy(dres_hbm.at[at, :], dres_ref.at[at, :], sems.at[i])
        for i, at in enumerate(spans)
    ]
    for read in reads:
        read.start()
    groups = rows // LANES
    acc = jnp.zeros((groups * width, LANES), F32)
    for index, back_ref in zip(pair_lists(rows_ref), (b0_ref, b1_ref, b2_ref, b3_ref)):
        acc += dot(spread(back_ref[...], index // LANES, groups), onehot(index & (LANES - 1)), NT)
    dproj = own_ref[...] + unstacked(acc, width)
    dpre = (dproj * silu_grad(pre_ref[...])).astype(BF16)
    for i, (at, read) in enumerate(zip(spans, reads)):
        down_term = dot(dpre[:, i * block : (i + 1) * block], down_ref[...], TN)
        read.wait()
        out_ref[at, :] = (dot(dres_ref[at, :], weight_ref[...], NT) + down_term).astype(BF16)


def edge_gradient(own, backs, outgoing, pre, weight, down_t, dres):
    rows, inner = dres.shape
    operands = (own, *backs, outgoing, pre, weight, down_t)
    return pl.pallas_call(
        edge_kernel,
        in_specs=[VMEM] * len(operands) + [HBM],
        out_specs=VMEM,
        out_shape=jax.ShapeDtypeStruct((rows, inner), BF16),
        scratch_shapes=[
            pltpu.VMEM((rows, inner), BF16),
            pltpu.SemaphoreType.DMA((rows // min(rows, LANES),)),
        ],
        compiler_params=limits(),
        cost_estimate=cost(4 * rows * inner * (inner + down_t.shape[0])),
        name="edge_gradient",
    )(*operands, *in_hbm(dres))


def finish_kernel(
    offsets, mine_ref, other_ref, residual_ref, down_ref, up_ref, basis_ref, all_ref, part_ref
):
    upper = lax.axis_index("brick") % 2
    slab = lax.axis_index("slab")
    half = residual_ref.shape[0] // 2
    step = half // len(offsets)
    columns = blocks_of(residual_ref.shape[1])
    block = mine_ref.shape[0] // len(offsets)
    tail = len(columns) * step
    share = block - tail
    for source, side in ((mine_ref, upper), (other_ref, 1 - upper)):
        for i, offset in enumerate(offsets):
            place = pl.ds(side * half + (slab ^ offset) * step, step)
            for c, column in enumerate(columns):
                at = pl.ds(i * block + c * step, step)
                residual_ref[place, column] = source[at, :].astype(F32)
            place = pl.ds((side * len(offsets) + (slab ^ offset)) * share, share)
            part_ref[place, :] = source[pl.ds(i * block + tail, share), :].astype(F32)
    rows, inner = all_ref.shape[0] // 2, down_ref.shape[1]
    for side in range(2):
        for c, column in enumerate(blocks_of(all_ref.shape[1])):
            at = pl.ds(side * len(offsets) * share + c * rows, rows)
            all_ref[pl.ds(side * rows, rows), column] = part_ref[at, :]
    down_ref[...] = all_ref[:, :inner]
    up_ref[...] = all_ref[:, inner : 2 * inner]
    nbasis, width = basis_ref.shape
    basis_ref[...] = all_ref[:nbasis, 2 * inner : 2 * inner + width]


def finish(offsets, mine, other, shared, inner, width, nbasis):
    return pl.pallas_call(
        lambda *refs: finish_kernel(offsets, *refs),
        in_specs=[VMEM] * 2,
        out_specs=[VMEM] * 4,
        out_shape=[
            jax.ShapeDtypeStruct((inner, inner), F32),
            jax.ShapeDtypeStruct((width, inner), F32),
            jax.ShapeDtypeStruct((width, inner), F32),
            jax.ShapeDtypeStruct((nbasis, width), F32),
        ],
        scratch_shapes=[
            pltpu.VMEM((width, 2 * inner + 128), F32),
            pltpu.VMEM((2 * shared, 128), F32),
        ],
        compiler_params=limits(),
        name="finish",
    )(mine, other)


def swapped(value, axis, offset):
    return lax.ppermute(value, axis, [(i, i ^ offset) for i in range(lax.axis_size(axis))])


def groups_of(axis, first):
    low, groups = first, []
    while low < lax.axis_size(axis):
        members = min(4, lax.axis_size(axis) // low)
        groups.append((low, members))
        low *= members
    return groups


def total_of(parts):
    return sum(part.astype(F32) for part in parts).astype(BF16)


def scattered_sum(values, axis, low, members, riders):
    digit = (lax.axis_index(axis) // low) % members

    def piece(value, k):
        rows = value.shape[0] // members
        return lax.dynamic_slice_in_dim(value, (digit ^ k) * rows, rows, 0)

    sums = [[piece(value, 0)] for value in values]
    arrived = {}
    for k in range(members - 1, 0, -1):
        sent = [piece(value, k) for value in values] + riders.get(k, [])
        received = swapped(jnp.concatenate(sent, axis=0), axis, k * low)
        start = 0
        for total in sums:
            total.append(received[start : start + total[0].shape[0]])
            start += total[0].shape[0]
        arrived[k] = received[start:]
    return [total_of(total) for total in sums], arrived


def exchanged(value, axis, low, members):
    return {k * low: swapped(value, axis, k * low) for k in range(members - 1, 0, -1)}


def shards(
    embed,
    cotangent,
    basis,
    triplet_row_index,
    triplet_slot_count,
    outgoing_edge_rows,
    residual_weight,
    down_weight,
    up_weight,
    basis_weight,
):
    rows, inner = embed.shape
    trips, nbasis = basis.shape[:2]

    *sends, embed_v, outgoing_v, weight_v = select(embed, outgoing_edge_rows, residual_weight)
    ghosts = pair_exchange(sends)
    basis = basis.reshape(trips * nbasis, rows)
    down_v, index_v, count_v, dres, mine, other, pre, weights = residual(
        embed_v,
        weight_v,
        cotangent,
        basis,
        basis_weight,
        down_weight.T,
        triplet_row_index,
        triplet_slot_count.reshape(1, rows),
    )
    share = total_of([mine, swapped(other, "brick", 1)])

    own, first, second, last, mine, other = triplets(
        pre,
        embed_v,
        down_v,
        ghosts,
        basis,
        index_v,
        count_v,
        up_weight,
        cotangent,
        weights,
    )
    received = swapped(other, "brick", 1)
    shared = mine.shape[0]
    mine = total_of([mine, received[:shared]])
    ring = lax.axis_size("slab")
    riders = {1: [first]}
    if ring == 4:
        riders[3] = [second]
    backs = [None, None, received[shared:], paired(last, "brick", 1)]
    slab_groups = groups_of("slab", 1)
    for low, members in reversed(slab_groups):
        (share, mine), arrived = scattered_sum(
            [share, mine], "slab", low, members, riders if low == 1 else {}
        )
    backs[0] = arrived[1]
    backs[1] = arrived[3] if ring == 4 else paired(second, "slab", 1)
    edge_grad = edge_gradient(own, backs, outgoing_v, pre, weight_v, down_v, dres)

    value = jnp.concatenate([share, mine], axis=0)
    for low, members in groups_of("brick", 2):
        value = total_of([value, *exchanged(value, "brick", low, members).values()])
    value, edge_grad = lax.optimization_barrier((value, edge_grad))
    pieces = {0: value}
    for low, members in slab_groups:
        known = sorted(pieces)
        value = jnp.concatenate([pieces[o] for o in known], axis=0)
        for k, other in exchanged(value, "slab", low, members).items():
            for i, offset in enumerate(known):
                step = pieces[offset].shape[0]
                pieces[offset ^ k] = other[i * step : (i + 1) * step]
    value = jnp.concatenate([pieces[o] for o in sorted(pieces)], axis=0)
    residual_grad, down_grad, up_grad, basis_grad = finish(
        sorted(pieces), value, swapped(value, "brick", 1), shared, inner, pre.shape[0], nbasis
    )
    return edge_grad, residual_grad, down_grad.T, up_grad, basis_grad


def solution(mesh):
    both = P(AXES, None)
    in_specs = (both, both, P(None, None, AXES), P(None, AXES), P(AXES), P(None, AXES)) + (P(),) * 4
    out_specs = (both, P(), P(), P(), P())
    return jax.shard_map(shards, mesh=mesh, in_specs=in_specs, out_specs=out_specs, check_vma=False)
```

```python
import jax
import jax.numpy as jnp
from jax import lax
from jax.experimental import pallas as pl
from jax.experimental.pallas import tpu as pltpu
from jax.sharding import PartitionSpec as P

AXES = ("slab", "brick")
LANES = 256
F32 = jnp.float32
BF16 = jnp.bfloat16
NN = ((1,), (0,))
NT = ((1,), (1,))
TN = ((0,), (0,))
VMEM = pl.BlockSpec(memory_space=pltpu.VMEM)
HBM = pl.BlockSpec(memory_space=pltpu.HBM)


def dot(a, b, dims, precision=None):
    return lax.dot_general(a, b, (dims, ((), ())), precision=precision, preferred_element_type=F32)


def like(*arrays):
    return [jax.ShapeDtypeStruct(a.shape, a.dtype) for a in arrays]


def in_hbm(*arrays):
    return [pltpu.with_memory_space_constraint(a, pltpu.HBM) for a in arrays]


def limits():
    return pltpu.CompilerParams(vmem_limit_bytes=30 * 2**20)


def cost(flops):
    return pl.CostEstimate(flops=flops, bytes_accessed=0, transcendentals=0)


def in_vmem(*arrays):
    return [pltpu.VMEM(a.shape, a.dtype) for a in arrays]


def blocks_of(width):
    return [pl.ds(start, 128) for start in range(0, width, 128)]


def sigmoid(value):
    return 1.0 / (1.0 + jnp.exp(-value))


def silu_grad(value):
    sig = sigmoid(value)
    return sig * (1.0 + value * (1.0 - sig))


def parity(axis):
    return lax.axis_index(axis) % 2 == 1


def onehot(low):
    rows = lax.broadcasted_iota(jnp.int32, (LANES, low.shape[1]), 0).astype(jnp.int16)
    return jnp.where(rows == low.astype(jnp.int16), jnp.ones((), BF16), jnp.zeros((), BF16))


def stacked(table):
    return jnp.concatenate(
        [table[:, g * LANES : (g + 1) * LANES] for g in range(table.shape[1] // LANES)], axis=0
    )


def unstacked(blocks, width):
    return jnp.concatenate(
        [blocks[g * width : (g + 1) * width] for g in range(blocks.shape[0] // width)], axis=1
    )


def chosen(blocks, high, width):
    total = jnp.zeros((width, blocks.shape[1]), F32)
    for g in range(blocks.shape[0] // width):
        total = jnp.where(high == g, blocks[g * width : (g + 1) * width], total)
    return total


def spread(values, high, groups):
    zero = jnp.zeros_like(values)
    return jnp.concatenate([jnp.where(high == g, values, zero) for g in range(groups)], axis=0)


def pair_lists(rows_ref):
    lists = []
    for first, axis in ((0, "slab"), (2, "brick")):
        odd = parity(axis)
        up, down = rows_ref[first : first + 1, :], rows_ref[first + 1 : first + 2, :]
        lists += [jnp.where(odd, down, up), jnp.where(odd, up, down)]
    return lists


def paired(value, axis, first):
    count = lax.axis_size(axis)
    pairs = []
    for i in range(first, count, 2):
        j = (i + 1) % count
        pairs += [(i, j), (j, i)]
    return lax.ppermute(value, axis, pairs)


def pair_exchange(values):
    spots = (("slab", 0), ("slab", 1), ("brick", 0), ("brick", 1))
    sent = {k: paired(values[k], *spots[k]) for k in (3, 1, 0, 2)}
    return [sent[k] for k in range(4)]


def select_kernel(
    embed_ref, rows_ref, weight_ref, s0, s1, s2, s3, embed_v, rows_v, weight_v, sems
):
    block = min(embed_ref.shape[0], LANES)
    spans = [pl.ds(start, block) for start in range(0, embed_ref.shape[0], block)]
    reads = [
        pltpu.make_async_copy(embed_ref.at[at, :], embed_v.at[at, :], sems.at[2 + i])
        for i, at in enumerate(spans)
    ]
    copies = [
        pltpu.make_async_copy(rows_ref, rows_v, sems.at[0]),
        pltpu.make_async_copy(weight_ref, weight_v, sems.at[1]),
    ]
    for copy in (copies[0], *reads, copies[1]):
        copy.start()
    copies[0].wait()
    rows = embed_v.shape[0]
    hots = []
    for index in pair_lists(rows_v):
        ghost = index.shape[1]
        column = jnp.broadcast_to(index.astype(F32), (128, ghost)).T
        wide = jnp.concatenate([column] * (rows // 128), axis=1).astype(jnp.int32).astype(jnp.int16)
        spots = lax.broadcasted_iota(jnp.int32, (ghost, rows), 1).astype(jnp.int16)
        hots.append(jnp.where(spots == wide, jnp.ones((), BF16), jnp.zeros((), BF16)))
    hot = jnp.concatenate(hots, axis=0)
    total = jnp.zeros((hot.shape[0], embed_v.shape[1]), F32)
    for i, (at, read) in enumerate(zip(spans, reads)):
        read.wait()
        total = total + dot(hot[:, i * block : (i + 1) * block], embed_v[at, :], NN)
    ghost = s0.shape[0]
    for i, send_ref in enumerate((s0, s1, s2, s3)):
        send_ref[...] = total[i * ghost : (i + 1) * ghost].astype(BF16)
    copies[1].wait()


def select(embed, outgoing, weight):
    rows = embed.shape[0]
    ghost = jax.ShapeDtypeStruct((outgoing.shape[1], embed.shape[1]), BF16)
    return pl.pallas_call(
        select_kernel,
        in_specs=[HBM] * 3,
        out_specs=[VMEM] * 7,
        out_shape=in_vmem(*[ghost] * 4, embed, outgoing, weight),
        scratch_shapes=[pltpu.SemaphoreType.DMA((2 + rows // min(rows, LANES),))],
        compiler_params=limits(),
        name="select",
    )(*in_hbm(embed, outgoing, weight))


def residual_kernel(embed_ref, weight_ref, cotangent_ref, basis_hbm, bw_hbm, *refs):
    count = (len(refs) - 11) // 2
    sources, targets = refs[:count], refs[count : 2 * count]
    dres_ref, mine_ref, other_ref, pre_ref, slots_ref = refs[2 * count : 2 * count + 5]
    cotangent_v, dres_v, grad_ref, basis_ref, bw_ref, sems = refs[2 * count + 5 :]
    rows = embed_ref.shape[0]
    block = min(rows, LANES)
    spans = [pl.ds(start, block) for start in range(0, rows, block)]
    reads = [
        pltpu.make_async_copy(cotangent_ref.at[at, :], cotangent_v.at[at, :], sems.at[i])
        for i, at in enumerate(spans)
    ]
    writes = [
        pltpu.make_async_copy(dres_v.at[at, :], dres_ref.at[at, :], sems.at[len(spans) + i])
        for i, at in enumerate(spans)
    ]
    copies = [
        pltpu.make_async_copy(source, target, sems.at[2 * len(spans) + i])
        for i, (source, target) in enumerate(
            zip((*sources, basis_hbm, bw_hbm), (*targets, basis_ref, bw_ref))
        )
    ]
    for copy in reads + copies:
        copy.start()
    for at, read, write in zip(spans, reads, writes):
        res_pre = dot(embed_ref[at, :], weight_ref[...], NN)
        grad = silu_grad(res_pre)
        read.wait()
        dres_v[at, :] = (cotangent_v[at, :].astype(F32) * grad).astype(BF16)
        write.start()
    copies[0].wait()
    pre_ref[...] = dot(targets[0][...], embed_ref[...], NT)
    grad_ref[...] = dot(embed_ref[...], dres_v[...], TN).astype(BF16)
    half = grad_ref.shape[0] // 2
    upper = lax.axis_index("brick") % 2
    columns = blocks_of(grad_ref.shape[1])
    step = half // lax.axis_size("slab")
    for part in range(half // step):
        for c, column in enumerate(columns):
            to = pl.ds((part * len(columns) + c) * step, step)
            mine_ref[to, :] = grad_ref[pl.ds(upper * half + part * step, step), column]
            other_ref[to, :] = grad_ref[pl.ds((1 - upper) * half + part * step, step), column]
    for copy in copies[1:]:
        copy.wait()
    nbasis, width = bw_ref.shape
    span = basis_ref.shape[0]
    trips = span // nbasis
    fold = jnp.where(
        lax.broadcasted_iota(jnp.int32, (nbasis, span), 1) % nbasis
        == lax.broadcasted_iota(jnp.int32, (nbasis, span), 0),
        1.0,
        0.0,
    )
    wide = dot(bw_ref[...], fold.astype(BF16), TN).astype(BF16)
    own_slot = lax.broadcasted_iota(jnp.int32, (trips, width, span), 0) == (
        lax.broadcasted_iota(jnp.int32, (trips, width, span), 2) // nbasis
    )
    diagonal = jnp.where(own_slot, wide[None], jnp.zeros((), BF16)).reshape(trips * width, span)
    slots_ref[...] = dot(diagonal, basis_ref[...], NN)

    for copy in writes:
        copy.wait()


def residual(embed, weight, cotangent, basis, basis_weight, down_t, *staged):
    staged = (down_t, *staged)
    width, rows = down_t.shape[0], embed.shape[0]
    trips = basis.shape[0] // basis_weight.shape[0]
    half = jax.ShapeDtypeStruct((weight.size // 256, 128), BF16)
    blocks = embed.shape[0] // min(embed.shape[0], LANES)
    return pl.pallas_call(
        residual_kernel,
        in_specs=[VMEM] * 2 + [HBM] * (3 + len(staged)),
        out_specs=[VMEM] * len(staged) + [HBM] + [VMEM] * 4,
        out_shape=in_vmem(*staged)
        + [pltpu.HBM(embed.shape, BF16)]
        + in_vmem(half, half)
        + [pltpu.VMEM((width, rows), F32), pltpu.VMEM((trips * width, rows), F32)],
        scratch_shapes=[
            pltpu.VMEM(embed.shape, BF16),
            pltpu.VMEM(embed.shape, BF16),
            pltpu.VMEM(weight.shape, BF16),
            pltpu.VMEM(basis.shape, BF16),
            pltpu.VMEM(basis_weight.shape, BF16),
            pltpu.SemaphoreType.DMA((2 * blocks + len(staged) + 2,)),
        ],
        compiler_params=limits(),
        cost_estimate=cost(6 * embed.size * weight.shape[1]),
        name="residual",
    )(embed, weight, *in_hbm(cotangent, basis, basis_weight, *staged))


def triplet_kernel(
    pre_ref,
    embed_ref,
    down_ref,
    g1_ref,
    g3_ref,
    g0_ref,
    g2_ref,
    index_ref,
    count_ref,
    weight_ref,
    basis_hbm,
    cotangent_hbm,
    up_hbm,
    own_ref,
    t0_ref,
    t1_ref,
    t3_ref,
    mine_ref,
    other_ref,
    ghost_embed_ref,
    rest_ref,
    table_ref,
    hot_ref,
    picked_ref,
    tsum_ref,
    dt_ref,
    acc_ref,
    basis_ref,
    cotangent_ref,
    up_ref,
    sems,
):
    read_basis = pltpu.make_async_copy(basis_hbm, basis_ref, sems.at[0])
    read_cotangent = pltpu.make_async_copy(cotangent_hbm, cotangent_ref, sems.at[1])
    read_up = pltpu.make_async_copy(up_hbm, up_ref, sems.at[2])
    read_basis.start()
    read_cotangent.start()
    read_up.start()
    width, rows = pre_ref.shape
    trips = index_ref.shape[0]
    nbasis = basis_ref.shape[0] // trips
    own_groups = rows // LANES
    ghost = g0_ref.shape[0]
    for first, a_ref, b_ref, axis in ((0, g0_ref, g1_ref, "slab"), (2, g2_ref, g3_ref, "brick")):
        odd = parity(axis)
        a, b = a_ref[...], b_ref[...]
        ghost_embed_ref[first * ghost : (first + 1) * ghost, :] = jnp.where(odd, a, b)
        ghost_embed_ref[(first + 1) * ghost : (first + 2) * ghost, :] = jnp.where(odd, b, a)
    ghost_pre = dot(down_ref[...], ghost_embed_ref[...], NT)
    ghost_grad = silu_grad(ghost_pre)
    own_pre = pre_ref[...]
    table_ref[: own_groups * width, :] = stacked((own_pre * sigmoid(own_pre)).astype(BF16))
    table_ref[own_groups * width :, :] = stacked((ghost_pre * sigmoid(ghost_pre)).astype(BF16))
    groups = table_ref.shape[0] // width
    tiles = rows // LANES

    tsum_ref[...] = jnp.zeros_like(tsum_ref)

    def lookup(j, t):
        at = pl.ds(t * LANES, LANES)
        index = index_ref[pl.ds(j, 1), at]
        high = jnp.where(j < count_ref[:, at], index // LANES, -1)
        return at, index & (LANES - 1), high

    def forward(j, carry):
        for t in range(tiles):
            at, low, high = lookup(j, t)
            hot = onehot(low)
            hot_ref[j, :, at] = hot
            picked = chosen(dot(table_ref[...], hot, NN), high, width)
            picked_ref[j, :, at] = picked.astype(BF16)
            tsum_ref[:, at] += weight_ref[pl.ds(j * width, width), at] * picked
        return carry

    lax.fori_loop(0, trips, forward, 0, unroll=16)

    tsum = tsum_ref[...]
    sig = sigmoid(tsum)
    act = (tsum * sig).astype(BF16)
    read_basis.wait()
    read_cotangent.wait()
    read_up.wait()
    cotangent = cotangent_ref[...]
    inner = cotangent.shape[1]
    rest_ref[:, inner : 2 * inner] = dot(act, cotangent, NN).astype(BF16)
    dsum = dot(up_ref[...], cotangent, NT)
    dt_ref[...] = dsum * (sig * (1.0 + tsum * (1.0 - sig)))
    acc_ref[...] = jnp.zeros_like(acc_ref)

    def backward(step, carry):
        parts, dws, hots, bases = [], [], [], []
        for k in range(group):
            j = step * group + k
            for t in range(tiles):
                at, low, high = lookup(j, t)
                dt = dt_ref[:, at]
                dws.append((dt * picked_ref[j, :, at].astype(F32)).astype(BF16))
                terms = (dt * weight_ref[pl.ds(j * width, width), at]).astype(BF16)
                parts.append(spread(terms, high, groups))
            hots.append(hot_ref[j])
            bases.append(basis_ref[pl.ds(pl.multiple_of(j * nbasis, nbasis), nbasis), :])
        hot = jnp.concatenate(hots, axis=1)
        acc_ref[...] += dot(jnp.concatenate(parts, axis=1), hot, NT)
        slot_basis = jnp.concatenate(bases, axis=1)
        return carry + dot(slot_basis, jnp.concatenate(dws, axis=1), NT)

    group = 2 if trips % 2 == 0 else 1
    basis_grad = lax.fori_loop(
        0, trips // group, backward, jnp.zeros((nbasis, width), F32), unroll=4
    )

    own = unstacked(acc_ref[: own_groups * width, :], width)
    own_ref[...] = own
    ghost_terms = unstacked(acc_ref[own_groups * width :, :], width)
    sides = []
    for first, axis in ((0, "slab"), (2, "brick")):
        odd = parity(axis)
        prev = ghost_terms[:, first * ghost : (first + 1) * ghost].astype(BF16)
        following = ghost_terms[:, (first + 1) * ghost : (first + 2) * ghost].astype(BF16)
        sides += [jnp.where(odd, prev, following), jnp.where(odd, following, prev)]
    t0_ref[...], t1_ref[...], t3_ref[...] = sides[0], sides[1], sides[3]
    down_grad = dot((own * silu_grad(pre_ref[...])).astype(BF16), embed_ref[...], NN)
    down_grad += dot((ghost_terms * ghost_grad).astype(BF16), ghost_embed_ref[...], NN)
    rest_ref[:, :inner] = down_grad.astype(BF16)
    rest_ref[:, 2 * inner :] = jnp.zeros((width, rest_ref.shape[1] - 2 * inner), BF16)
    rest_ref[:nbasis, 2 * inner : 2 * inner + width] = basis_grad.astype(BF16)
    half = width // 2
    upper = lax.axis_index("brick") % 2
    columns = blocks_of(rest_ref.shape[1])
    for c, column in enumerate(columns):
        to = pl.ds(c * half, half)
        mine_ref[to, :] = rest_ref[pl.ds(upper * half, half), column]
        other_ref[to, :] = rest_ref[pl.ds((1 - upper) * half, half), column]
    used, total = len(columns) * half, mine_ref.shape[0]
    if used < total:
        mine_ref[used:, :] = jnp.zeros((total - used, 128), BF16)
        other_ref[used:total, :] = jnp.zeros((total - used, 128), BF16)
    for c, column in enumerate(blocks_of(ghost)):
        other_ref[pl.ds(total + c * width, width), :] = sides[2][:, column]


def triplets(
    pre, embed, down_t, ghosts, basis, index, count, up_weight, cotangent, weights
):
    width, rows = pre.shape
    trips = index.shape[0]
    ghost, inner = ghosts[0].shape
    groups = (rows + 4 * ghost) // LANES
    ordered = [ghosts[k] for k in (1, 3, 0, 2)]
    operands = (pre, embed, down_t, *ordered, index, count, weights)
    unit = 16 * lax.axis_size("slab")
    total = 2 * inner + 128
    shared = -(-(width * total // 256) // unit) * unit
    out_shape = (
        [pltpu.VMEM((width, rows), F32)]
        + [pltpu.VMEM((width, ghost), BF16)] * 3
        + [pltpu.VMEM((shared, 128), BF16), pltpu.VMEM((shared + width * ghost // 128, 128), BF16)]
    )
    return pl.pallas_call(
        triplet_kernel,
        in_specs=[VMEM] * len(operands) + [HBM] * 3,
        out_specs=[VMEM] * len(out_shape),
        out_shape=out_shape,
        scratch_shapes=[
            pltpu.VMEM((4 * ghost, inner), BF16),
            pltpu.VMEM((width, total), BF16),
            pltpu.VMEM((groups * width, LANES), BF16),
            pltpu.VMEM((trips, LANES, rows), BF16),
            pltpu.VMEM((trips, width, rows), BF16),
            pltpu.VMEM((width, rows), F32),
            pltpu.VMEM((width, rows), F32),
            pltpu.VMEM((groups * width, LANES), F32),
            pltpu.VMEM(basis.shape, BF16),
            pltpu.VMEM(cotangent.shape, BF16),
            pltpu.VMEM(up_weight.shape, BF16),
            pltpu.SemaphoreType.DMA((3,)),
        ],
        compiler_params=limits(),
        cost_estimate=cost(8 * trips * rows * width * (rows + 4 * ghost)),
        name="triplets",
    )(*operands, *in_hbm(basis, cotangent, up_weight))


def edge_kernel(
    own_ref,
    b0_ref,
    b1_ref,
    b2_ref,
    b3_ref,
    rows_ref,
    pre_ref,
    weight_ref,
    down_ref,
    dres_hbm,
    out_ref,
    dres_ref,
    sems,
):
    width, rows = own_ref.shape
    block = min(rows, LANES)
    spans = [pl.ds(start, block) for start in range(0, rows, block)]
    reads = [
        pltpu.make_async_copy(dres_hbm.at[at, :], dres_ref.at[at, :], sems.at[i])
        for i, at in enumerate(spans)
    ]
    for read in reads:
        read.start()
    groups = rows // LANES
    acc = jnp.zeros((groups * width, LANES), F32)
    for index, back_ref in zip(pair_lists(rows_ref), (b0_ref, b1_ref, b2_ref, b3_ref)):
        acc += dot(spread(back_ref[...], index // LANES, groups), onehot(index & (LANES - 1)), NT)
    dproj = own_ref[...] + unstacked(acc, width)
    dpre = (dproj * silu_grad(pre_ref[...])).astype(BF16)
    for i, (at, read) in enumerate(zip(spans, reads)):
        down_term = dot(dpre[:, i * block : (i + 1) * block], down_ref[...], TN)
        read.wait()
        out_ref[at, :] = (dot(dres_ref[at, :], weight_ref[...], NT) + down_term).astype(BF16)


def edge_gradient(own, backs, outgoing, pre, weight, down_t, dres):
    rows, inner = dres.shape
    operands = (own, *backs, outgoing, pre, weight, down_t)
    return pl.pallas_call(
        edge_kernel,
        in_specs=[VMEM] * len(operands) + [HBM],
        out_specs=VMEM,
        out_shape=jax.ShapeDtypeStruct((rows, inner), BF16),
        scratch_shapes=[
            pltpu.VMEM((rows, inner), BF16),
            pltpu.SemaphoreType.DMA((rows // min(rows, LANES),)),
        ],
        compiler_params=limits(),
        cost_estimate=cost(4 * rows * inner * (inner + down_t.shape[0])),
        name="edge_gradient",
    )(*operands, *in_hbm(dres))


def finish_kernel(
    offsets, mine_ref, other_ref, residual_ref, down_ref, up_ref, basis_ref, all_ref, part_ref
):
    upper = lax.axis_index("brick") % 2
    slab = lax.axis_index("slab")
    half = residual_ref.shape[0] // 2
    step = half // len(offsets)
    columns = blocks_of(residual_ref.shape[1])
    block = mine_ref.shape[0] // len(offsets)
    tail = len(columns) * step
    share = block - tail
    for source, side in ((mine_ref, upper), (other_ref, 1 - upper)):
        for i, offset in enumerate(offsets):
            place = pl.ds(side * half + (slab ^ offset) * step, step)
            for c, column in enumerate(columns):
                at = pl.ds(i * block + c * step, step)
                residual_ref[place, column] = source[at, :].astype(F32)
            place = pl.ds((side * len(offsets) + (slab ^ offset)) * share, share)
            part_ref[place, :] = source[pl.ds(i * block + tail, share), :].astype(F32)
    rows, inner = all_ref.shape[0] // 2, down_ref.shape[1]
    for side in range(2):
        for c, column in enumerate(blocks_of(all_ref.shape[1])):
            at = pl.ds(side * len(offsets) * share + c * rows, rows)
            all_ref[pl.ds(side * rows, rows), column] = part_ref[at, :]
    down_ref[...] = all_ref[:, :inner]
    up_ref[...] = all_ref[:, inner : 2 * inner]
    nbasis, width = basis_ref.shape
    basis_ref[...] = all_ref[:nbasis, 2 * inner : 2 * inner + width]


def finish(offsets, mine, other, shared, inner, width, nbasis):
    return pl.pallas_call(
        lambda *refs: finish_kernel(offsets, *refs),
        in_specs=[VMEM] * 2,
        out_specs=[VMEM] * 4,
        out_shape=[
            jax.ShapeDtypeStruct((inner, inner), F32),
            jax.ShapeDtypeStruct((width, inner), F32),
            jax.ShapeDtypeStruct((width, inner), F32),
            jax.ShapeDtypeStruct((nbasis, width), F32),
        ],
        scratch_shapes=[
            pltpu.VMEM((width, 2 * inner + 128), F32),
            pltpu.VMEM((2 * shared, 128), F32),
        ],
        compiler_params=limits(),
        name="finish",
    )(mine, other)


def swapped(value, axis, offset):
    return lax.ppermute(value, axis, [(i, i ^ offset) for i in range(lax.axis_size(axis))])


def groups_of(axis, first):
    low, groups = first, []
    while low < lax.axis_size(axis):
        members = min(4, lax.axis_size(axis) // low)
        groups.append((low, members))
        low *= members
    return groups


def total_of(parts):
    return sum(part.astype(F32) for part in parts).astype(BF16)


def scattered_sum(values, axis, low, members, riders):
    digit = (lax.axis_index(axis) // low) % members

    def piece(value, k):
        rows = value.shape[0] // members
        return lax.dynamic_slice_in_dim(value, (digit ^ k) * rows, rows, 0)

    sums = [[piece(value, 0)] for value in values]
    arrived = {}
    for k in range(members - 1, 0, -1):
        sent = [piece(value, k) for value in values] + riders.get(k, [])
        received = swapped(jnp.concatenate(sent, axis=0), axis, k * low)
        start = 0
        for total in sums:
            total.append(received[start : start + total[0].shape[0]])
            start += total[0].shape[0]
        arrived[k] = received[start:]
    return [total_of(total) for total in sums], arrived


def exchanged(value, axis, low, members):
    return {k * low: swapped(value, axis, k * low) for k in range(members - 1, 0, -1)}


def shards(
    embed,
    cotangent,
    basis,
    triplet_row_index,
    triplet_slot_count,
    outgoing_edge_rows,
    residual_weight,
    down_weight,
    up_weight,
    basis_weight,
):
    rows, inner = embed.shape
    trips, nbasis = basis.shape[:2]

    *sends, embed_v, outgoing_v, weight_v = select(embed, outgoing_edge_rows, residual_weight)
    ghosts = pair_exchange(sends)
    basis = basis.reshape(trips * nbasis, rows)
    down_v, index_v, count_v, dres, mine, other, pre, weights = residual(
        embed_v,
        weight_v,
        cotangent,
        basis,
        basis_weight,
        down_weight.T,
        triplet_row_index,
        triplet_slot_count.reshape(1, rows),
    )
    share = total_of([mine, swapped(other, "brick", 1)])

    own, first, second, last, mine, other = triplets(
        pre,
        embed_v,
        down_v,
        ghosts,
        basis,
        index_v,
        count_v,
        up_weight,
        cotangent,
        weights,
    )
    received = swapped(other, "brick", 1)
    shared = mine.shape[0]
    mine = total_of([mine, received[:shared]])
    ring = lax.axis_size("slab")
    riders = {1: [first]}
    if ring == 4:
        riders[3] = [second]
    backs = [None, None, received[shared:], paired(last, "brick", 1)]
    slab_groups = groups_of("slab", 1)
    for low, members in reversed(slab_groups):
        (share, mine), arrived = scattered_sum(
            [share, mine], "slab", low, members, riders if low == 1 else {}
        )
    backs[0] = arrived[1]
    backs[1] = arrived[3] if ring == 4 else paired(second, "slab", 1)
    edge_grad = edge_gradient(own, backs, outgoing_v, pre, weight_v, down_v, dres)

    value = jnp.concatenate([share, mine], axis=0)
    for low, members in groups_of("brick", 2):
        value = total_of([value, *exchanged(value, "brick", low, members).values()])
    value, edge_grad = lax.optimization_barrier((value, edge_grad))
    pieces = {0: value}
    for low, members in slab_groups:
        known = sorted(pieces)
        value = jnp.concatenate([pieces[o] for o in known], axis=0)
        for k, other in exchanged(value, "slab", low, members).items():
            for i, offset in enumerate(known):
                step = pieces[offset].shape[0]
                pieces[offset ^ k] = other[i * step : (i + 1) * step]
    value = jnp.concatenate([pieces[o] for o in sorted(pieces)], axis=0)
    residual_grad, down_grad, up_grad, basis_grad = finish(
        sorted(pieces), value, swapped(value, "brick", 1), shared, inner, pre.shape[0], nbasis
    )
    return edge_grad, residual_grad, down_grad.T, up_grad, basis_grad


def solution(mesh):
    both = P(AXES, None)
    in_specs = (both, both, P(None, None, AXES), P(None, AXES), P(AXES), P(None, AXES)) + (P(),) * 4
    out_specs = (both, P(), P(), P(), P())
    return jax.shard_map(shards, mesh=mesh, in_specs=in_specs, out_specs=out_specs, check_vma=False)
```

```python
import jax
import jax.numpy as jnp
from jax import lax
from jax.experimental import pallas as pl
from jax.experimental.pallas import tpu as pltpu
from jax.sharding import PartitionSpec as P

AXES = ("slab", "brick")
LANES = 256
F32 = jnp.float32
BF16 = jnp.bfloat16
NN = ((1,), (0,))
NT = ((1,), (1,))
TN = ((0,), (0,))
VMEM = pl.BlockSpec(memory_space=pltpu.VMEM)
HBM = pl.BlockSpec(memory_space=pltpu.HBM)


def dot(a, b, dims, precision=None):
    return lax.dot_general(a, b, (dims, ((), ())), precision=precision, preferred_element_type=F32)


def like(*arrays):
    return [jax.ShapeDtypeStruct(a.shape, a.dtype) for a in arrays]


def in_hbm(*arrays):
    return [pltpu.with_memory_space_constraint(a, pltpu.HBM) for a in arrays]


def limits():
    return pltpu.CompilerParams(vmem_limit_bytes=30 * 2**20)


def cost(flops):
    return pl.CostEstimate(flops=flops, bytes_accessed=0, transcendentals=0)


def in_vmem(*arrays):
    return [pltpu.VMEM(a.shape, a.dtype) for a in arrays]


def blocks_of(width):
    return [pl.ds(start, 128) for start in range(0, width, 128)]


def sigmoid(value):
    return 1.0 / (1.0 + jnp.exp(-value))


def silu_grad(value):
    sig = sigmoid(value)
    return sig * (1.0 + value * (1.0 - sig))


def parity(axis):
    return lax.axis_index(axis) % 2 == 1


def onehot(low):
    rows = lax.broadcasted_iota(jnp.int32, (LANES, low.shape[1]), 0).astype(jnp.int16)
    return jnp.where(rows == low.astype(jnp.int16), jnp.ones((), BF16), jnp.zeros((), BF16))


def stacked(table):
    return jnp.concatenate(
        [table[:, g * LANES : (g + 1) * LANES] for g in range(table.shape[1] // LANES)], axis=0
    )


def unstacked(blocks, width):
    return jnp.concatenate(
        [blocks[g * width : (g + 1) * width] for g in range(blocks.shape[0] // width)], axis=1
    )


def chosen(blocks, high, width):
    total = jnp.zeros((width, blocks.shape[1]), F32)
    for g in range(blocks.shape[0] // width):
        total = jnp.where(high == g, blocks[g * width : (g + 1) * width], total)
    return total


def spread(values, high, groups):
    zero = jnp.zeros_like(values)
    return jnp.concatenate([jnp.where(high == g, values, zero) for g in range(groups)], axis=0)


def pair_lists(rows_ref):
    lists = []
    for first, axis in ((0, "slab"), (2, "brick")):
        odd = parity(axis)
        up, down = rows_ref[first : first + 1, :], rows_ref[first + 1 : first + 2, :]
        lists += [jnp.where(odd, down, up), jnp.where(odd, up, down)]
    return lists


def paired(value, axis, first):
    count = lax.axis_size(axis)
    pairs = []
    for i in range(first, count, 2):
        j = (i + 1) % count
        pairs += [(i, j), (j, i)]
    return lax.ppermute(value, axis, pairs)


def pair_exchange(values):
    spots = (("slab", 0), ("slab", 1), ("brick", 0), ("brick", 1))
    sent = {k: paired(values[k], *spots[k]) for k in (3, 1, 0, 2)}
    return [sent[k] for k in range(4)]


def select_kernel(
    embed_ref, rows_ref, weight_ref, s0, s1, s2, s3, embed_v, rows_v, weight_v, sems
):
    block = min(embed_ref.shape[0], LANES)
    spans = [pl.ds(start, block) for start in range(0, embed_ref.shape[0], block)]
    reads = [
        pltpu.make_async_copy(embed_ref.at[at, :], embed_v.at[at, :], sems.at[2 + i])
        for i, at in enumerate(spans)
    ]
    copies = [
        pltpu.make_async_copy(rows_ref, rows_v, sems.at[0]),
        pltpu.make_async_copy(weight_ref, weight_v, sems.at[1]),
    ]
    for copy in (copies[0], *reads, copies[1]):
        copy.start()
    copies[0].wait()
    rows = embed_v.shape[0]
    hots = []
    for index in pair_lists(rows_v):
        ghost = index.shape[1]
        column = jnp.broadcast_to(index.astype(F32), (128, ghost)).T
        wide = jnp.concatenate([column] * (rows // 128), axis=1).astype(jnp.int32).astype(jnp.int16)
        spots = lax.broadcasted_iota(jnp.int32, (ghost, rows), 1).astype(jnp.int16)
        hots.append(jnp.where(spots == wide, jnp.ones((), BF16), jnp.zeros((), BF16)))
    hot = jnp.concatenate(hots, axis=0)
    total = jnp.zeros((hot.shape[0], embed_v.shape[1]), F32)
    for i, (at, read) in enumerate(zip(spans, reads)):
        read.wait()
        total = total + dot(hot[:, i * block : (i + 1) * block], embed_v[at, :], NN)
    ghost = s0.shape[0]
    for i, send_ref in enumerate((s0, s1, s2, s3)):
        send_ref[...] = total[i * ghost : (i + 1) * ghost].astype(BF16)
    copies[1].wait()


def select(embed, outgoing, weight):
    rows = embed.shape[0]
    ghost = jax.ShapeDtypeStruct((outgoing.shape[1], embed.shape[1]), BF16)
    return pl.pallas_call(
        select_kernel,
        in_specs=[HBM] * 3,
        out_specs=[VMEM] * 7,
        out_shape=in_vmem(*[ghost] * 4, embed, outgoing, weight),
        scratch_shapes=[pltpu.SemaphoreType.DMA((2 + rows // min(rows, LANES),))],
        compiler_params=limits(),
        name="select",
    )(*in_hbm(embed, outgoing, weight))


def residual_kernel(embed_ref, weight_ref, cotangent_ref, basis_hbm, bw_hbm, *refs):
    count = (len(refs) - 11) // 2
    sources, targets = refs[:count], refs[count : 2 * count]
    dres_ref, mine_ref, other_ref, pre_ref, slots_ref = refs[2 * count : 2 * count + 5]
    cotangent_v, dres_v, grad_ref, basis_ref, bw_ref, sems = refs[2 * count + 5 :]
    rows = embed_ref.shape[0]
    block = min(rows, LANES)
    spans = [pl.ds(start, block) for start in range(0, rows, block)]
    reads = [
        pltpu.make_async_copy(cotangent_ref.at[at, :], cotangent_v.at[at, :], sems.at[i])
        for i, at in enumerate(spans)
    ]
    writes = [
        pltpu.make_async_copy(dres_v.at[at, :], dres_ref.at[at, :], sems.at[len(spans) + i])
        for i, at in enumerate(spans)
    ]
    copies = [
        pltpu.make_async_copy(source, target, sems.at[2 * len(spans) + i])
        for i, (source, target) in enumerate(
            zip((*sources, basis_hbm, bw_hbm), (*targets, basis_ref, bw_ref))
        )
    ]
    for copy in reads + copies:
        copy.start()
    for at, read, write in zip(spans, reads, writes):
        res_pre = dot(embed_ref[at, :], weight_ref[...], NN)
        grad = silu_grad(res_pre)
        read.wait()
        dres_v[at, :] = (cotangent_v[at, :].astype(F32) * grad).astype(BF16)
        write.start()
    copies[0].wait()
    pre_ref[...] = dot(targets[0][...], embed_ref[...], NT)
    grad_ref[...] = dot(embed_ref[...], dres_v[...], TN).astype(BF16)
    half = grad_ref.shape[0] // 2
    upper = lax.axis_index("brick") % 2
    columns = blocks_of(grad_ref.shape[1])
    step = half // lax.axis_size("slab")
    for part in range(half // step):
        for c, column in enumerate(columns):
            to = pl.ds((part * len(columns) + c) * step, step)
            mine_ref[to, :] = grad_ref[pl.ds(upper * half + part * step, step), column]
            other_ref[to, :] = grad_ref[pl.ds((1 - upper) * half + part * step, step), column]
    for copy in copies[1:]:
        copy.wait()
    nbasis, width = bw_ref.shape
    span = basis_ref.shape[0]
    trips = span // nbasis
    fold = jnp.where(
        lax.broadcasted_iota(jnp.int32, (nbasis, span), 1) % nbasis
        == lax.broadcasted_iota(jnp.int32, (nbasis, span), 0),
        1.0,
        0.0,
    )
    wide = dot(bw_ref[...], fold.astype(BF16), TN).astype(BF16)
    own_slot = lax.broadcasted_iota(jnp.int32, (trips, width, span), 0) == (
        lax.broadcasted_iota(jnp.int32, (trips, width, span), 2) // nbasis
    )
    diagonal = jnp.where(own_slot, wide[None], jnp.zeros((), BF16)).reshape(trips * width, span)
    slots_ref[...] = dot(diagonal, basis_ref[...], NN)

    for copy in writes:
        copy.wait()


def residual(embed, weight, cotangent, basis, basis_weight, down_t, *staged):
    staged = (down_t, *staged)
    width, rows = down_t.shape[0], embed.shape[0]
    trips = basis.shape[0] // basis_weight.shape[0]
    half = jax.ShapeDtypeStruct((weight.size // 256, 128), BF16)
    blocks = embed.shape[0] // min(embed.shape[0], LANES)
    return pl.pallas_call(
        residual_kernel,
        in_specs=[VMEM] * 2 + [HBM] * (3 + len(staged)),
        out_specs=[VMEM] * len(staged) + [HBM] + [VMEM] * 4,
        out_shape=in_vmem(*staged)
        + [pltpu.HBM(embed.shape, BF16)]
        + in_vmem(half, half)
        + [pltpu.VMEM((width, rows), F32), pltpu.VMEM((trips * width, rows), F32)],
        scratch_shapes=[
            pltpu.VMEM(embed.shape, BF16),
            pltpu.VMEM(embed.shape, BF16),
            pltpu.VMEM(weight.shape, BF16),
            pltpu.VMEM(basis.shape, BF16),
            pltpu.VMEM(basis_weight.shape, BF16),
            pltpu.SemaphoreType.DMA((2 * blocks + len(staged) + 2,)),
        ],
        compiler_params=limits(),
        cost_estimate=cost(6 * embed.size * weight.shape[1]),
        name="residual",
    )(embed, weight, *in_hbm(cotangent, basis, basis_weight, *staged))


def triplet_kernel(
    pre_ref,
    embed_ref,
    down_ref,
    g1_ref,
    g3_ref,
    g0_ref,
    g2_ref,
    index_ref,
    count_ref,
    weight_ref,
    basis_hbm,
    cotangent_hbm,
    up_hbm,
    own_ref,
    t0_ref,
    t1_ref,
    t3_ref,
    mine_ref,
    other_ref,
    ghost_embed_ref,
    rest_ref,
    table_ref,
    hot_ref,
    picked_ref,
    tsum_ref,
    dt_ref,
    acc_ref,
    basis_ref,
    cotangent_ref,
    up_ref,
    sems,
):
    read_basis = pltpu.make_async_copy(basis_hbm, basis_ref, sems.at[0])
    read_cotangent = pltpu.make_async_copy(cotangent_hbm, cotangent_ref, sems.at[1])
    read_up = pltpu.make_async_copy(up_hbm, up_ref, sems.at[2])
    read_basis.start()
    read_cotangent.start()
    read_up.start()
    width, rows = pre_ref.shape
    trips = index_ref.shape[0]
    nbasis = basis_ref.shape[0] // trips
    own_groups = rows // LANES
    ghost = g0_ref.shape[0]
    for first, a_ref, b_ref, axis in ((0, g0_ref, g1_ref, "slab"), (2, g2_ref, g3_ref, "brick")):
        odd = parity(axis)
        a, b = a_ref[...], b_ref[...]
        ghost_embed_ref[first * ghost : (first + 1) * ghost, :] = jnp.where(odd, a, b)
        ghost_embed_ref[(first + 1) * ghost : (first + 2) * ghost, :] = jnp.where(odd, b, a)
    ghost_pre = dot(down_ref[...], ghost_embed_ref[...], NT)
    ghost_grad = silu_grad(ghost_pre)
    own_pre = pre_ref[...]
    table_ref[: own_groups * width, :] = stacked((own_pre * sigmoid(own_pre)).astype(BF16))
    table_ref[own_groups * width :, :] = stacked((ghost_pre * sigmoid(ghost_pre)).astype(BF16))
    groups = table_ref.shape[0] // width
    tiles = rows // LANES

    tsum_ref[...] = jnp.zeros_like(tsum_ref)

    def lookup(j, t):
        at = pl.ds(t * LANES, LANES)
        index = index_ref[pl.ds(j, 1), at]
        high = jnp.where(j < count_ref[:, at], index // LANES, -1)
        return at, index & (LANES - 1), high

    def forward(j, carry):
        for t in range(tiles):
            at, low, high = lookup(j, t)
            hot = onehot(low)
            hot_ref[j, :, at] = hot
            picked = chosen(dot(table_ref[...], hot, NN), high, width)
            picked_ref[j, :, at] = picked.astype(BF16)
            tsum_ref[:, at] += weight_ref[pl.ds(j * width, width), at] * picked
        return carry

    lax.fori_loop(0, trips, forward, 0, unroll=16)

    tsum = tsum_ref[...]
    sig = sigmoid(tsum)
    act = (tsum * sig).astype(BF16)
    read_basis.wait()
    read_cotangent.wait()
    read_up.wait()
    cotangent = cotangent_ref[...]
    inner = cotangent.shape[1]
    rest_ref[:, inner : 2 * inner] = dot(act, cotangent, NN).astype(BF16)
    dsum = dot(up_ref[...], cotangent, NT)
    dt_ref[...] = dsum * (sig * (1.0 + tsum * (1.0 - sig)))
    acc_ref[...] = jnp.zeros_like(acc_ref)

    def backward(step, carry):
        parts, dws, hots, bases = [], [], [], []
        for k in range(group):
            j = step * group + k
            for t in range(tiles):
                at, low, high = lookup(j, t)
                dt = dt_ref[:, at]
                dws.append((dt * picked_ref[j, :, at].astype(F32)).astype(BF16))
                terms = (dt * weight_ref[pl.ds(j * width, width), at]).astype(BF16)
                parts.append(spread(terms, high, groups))
            hots.append(hot_ref[j])
            bases.append(basis_ref[pl.ds(pl.multiple_of(j * nbasis, nbasis), nbasis), :])
        hot = jnp.concatenate(hots, axis=1)
        acc_ref[...] += dot(jnp.concatenate(parts, axis=1), hot, NT)
        slot_basis = jnp.concatenate(bases, axis=1)
        return carry + dot(slot_basis, jnp.concatenate(dws, axis=1), NT)

    group = 2 if trips % 2 == 0 else 1
    basis_grad = lax.fori_loop(
        0, trips // group, backward, jnp.zeros((nbasis, width), F32), unroll=4
    )

    own = unstacked(acc_ref[: own_groups * width, :], width)
    own_ref[...] = own
    ghost_terms = unstacked(acc_ref[own_groups * width :, :], width)
    sides = []
    for first, axis in ((0, "slab"), (2, "brick")):
        odd = parity(axis)
        prev = ghost_terms[:, first * ghost : (first + 1) * ghost].astype(BF16)
        following = ghost_terms[:, (first + 1) * ghost : (first + 2) * ghost].astype(BF16)
        sides += [jnp.where(odd, prev, following), jnp.where(odd, following, prev)]
    t0_ref[...], t1_ref[...], t3_ref[...] = sides[0], sides[1], sides[3]
    down_grad = dot((own * silu_grad(pre_ref[...])).astype(BF16), embed_ref[...], NN)
    down_grad += dot((ghost_terms * ghost_grad).astype(BF16), ghost_embed_ref[...], NN)
    rest_ref[:, :inner] = down_grad.astype(BF16)
    rest_ref[:, 2 * inner :] = jnp.zeros((width, rest_ref.shape[1] - 2 * inner), BF16)
    rest_ref[:nbasis, 2 * inner : 2 * inner + width] = basis_grad.astype(BF16)
    half = width // 2
    upper = lax.axis_index("brick") % 2
    columns = blocks_of(rest_ref.shape[1])
    for c, column in enumerate(columns):
        to = pl.ds(c * half, half)
        mine_ref[to, :] = rest_ref[pl.ds(upper * half, half), column]
        other_ref[to, :] = rest_ref[pl.ds((1 - upper) * half, half), column]
    used, total = len(columns) * half, mine_ref.shape[0]
    if used < total:
        mine_ref[used:, :] = jnp.zeros((total - used, 128), BF16)
        other_ref[used:total, :] = jnp.zeros((total - used, 128), BF16)
    for c, column in enumerate(blocks_of(ghost)):
        other_ref[pl.ds(total + c * width, width), :] = sides[2][:, column]


def triplets(
    pre, embed, down_t, ghosts, basis, index, count, up_weight, cotangent, weights
):
    width, rows = pre.shape
    trips = index.shape[0]
    ghost, inner = ghosts[0].shape
    groups = (rows + 4 * ghost) // LANES
    ordered = [ghosts[k] for k in (1, 3, 0, 2)]
    operands = (pre, embed, down_t, *ordered, index, count, weights)
    unit = 16 * lax.axis_size("slab")
    total = 2 * inner + 128
    shared = -(-(width * total // 256) // unit) * unit
    out_shape = (
        [pltpu.VMEM((width, rows), F32)]
        + [pltpu.VMEM((width, ghost), BF16)] * 3
        + [pltpu.VMEM((shared, 128), BF16), pltpu.VMEM((shared + width * ghost // 128, 128), BF16)]
    )
    return pl.pallas_call(
        triplet_kernel,
        in_specs=[VMEM] * len(operands) + [HBM] * 3,
        out_specs=[VMEM] * len(out_shape),
        out_shape=out_shape,
        scratch_shapes=[
            pltpu.VMEM((4 * ghost, inner), BF16),
            pltpu.VMEM((width, total), BF16),
            pltpu.VMEM((groups * width, LANES), BF16),
            pltpu.VMEM((trips, LANES, rows), BF16),
            pltpu.VMEM((trips, width, rows), BF16),
            pltpu.VMEM((width, rows), F32),
            pltpu.VMEM((width, rows), F32),
            pltpu.VMEM((groups * width, LANES), F32),
            pltpu.VMEM(basis.shape, BF16),
            pltpu.VMEM(cotangent.shape, BF16),
            pltpu.VMEM(up_weight.shape, BF16),
            pltpu.SemaphoreType.DMA((3,)),
        ],
        compiler_params=limits(),
        cost_estimate=cost(8 * trips * rows * width * (rows + 4 * ghost)),
        name="triplets",
    )(*operands, *in_hbm(basis, cotangent, up_weight))


def edge_kernel(
    own_ref,
    b0_ref,
    b1_ref,
    b2_ref,
    b3_ref,
    rows_ref,
    pre_ref,
    weight_ref,
    down_ref,
    dres_hbm,
    out_ref,
    dres_ref,
    sems,
):
    width, rows = own_ref.shape
    block = min(rows, LANES)
    spans = [pl.ds(start, block) for start in range(0, rows, block)]
    reads = [
        pltpu.make_async_copy(dres_hbm.at[at, :], dres_ref.at[at, :], sems.at[i])
        for i, at in enumerate(spans)
    ]
    for read in reads:
        read.start()
    groups = rows // LANES
    acc = jnp.zeros((groups * width, LANES), F32)
    for index, back_ref in zip(pair_lists(rows_ref), (b0_ref, b1_ref, b2_ref, b3_ref)):
        acc += dot(spread(back_ref[...], index // LANES, groups), onehot(index & (LANES - 1)), NT)
    dproj = own_ref[...] + unstacked(acc, width)
    dpre = (dproj * silu_grad(pre_ref[...])).astype(BF16)
    for i, (at, read) in enumerate(zip(spans, reads)):
        down_term = dot(dpre[:, i * block : (i + 1) * block], down_ref[...], TN)
        read.wait()
        out_ref[at, :] = (dot(dres_ref[at, :], weight_ref[...], NT) + down_term).astype(BF16)


def edge_gradient(own, backs, outgoing, pre, weight, down_t, dres):
    rows, inner = dres.shape
    operands = (own, *backs, outgoing, pre, weight, down_t)
    return pl.pallas_call(
        edge_kernel,
        in_specs=[VMEM] * len(operands) + [HBM],
        out_specs=VMEM,
        out_shape=jax.ShapeDtypeStruct((rows, inner), BF16),
        scratch_shapes=[
            pltpu.VMEM((rows, inner), BF16),
            pltpu.SemaphoreType.DMA((rows // min(rows, LANES),)),
        ],
        compiler_params=limits(),
        cost_estimate=cost(4 * rows * inner * (inner + down_t.shape[0])),
        name="edge_gradient",
    )(*operands, *in_hbm(dres))


def finish_kernel(offsets, *refs):
    count = len(offsets)
    kept, sent = refs[:count], refs[count : 2 * count]
    residual_ref, down_ref, up_ref, basis_ref, all_ref, part_ref = refs[2 * count :]
    upper = lax.axis_index("brick") % 2
    slab = lax.axis_index("slab")
    half = residual_ref.shape[0] // 2
    step = half // len(offsets)
    columns = blocks_of(residual_ref.shape[1])
    block = kept[0].shape[0]
    tail = len(columns) * step
    share = block - tail
    for sources, side in ((kept, upper), (sent, 1 - upper)):
        for source, offset in zip(sources, offsets):
            place = pl.ds(side * half + (slab ^ offset) * step, step)
            for c, column in enumerate(columns):
                at = pl.ds(c * step, step)
                residual_ref[place, column] = source[at, :].astype(F32)
            place = pl.ds((side * len(offsets) + (slab ^ offset)) * share, share)
            part_ref[place, :] = source[pl.ds(tail, share), :].astype(F32)
    rows, inner = all_ref.shape[0] // 2, down_ref.shape[1]
    for side in range(2):
        for c, column in enumerate(blocks_of(all_ref.shape[1])):
            at = pl.ds(side * len(offsets) * share + c * rows, rows)
            all_ref[pl.ds(side * rows, rows), column] = part_ref[at, :]
    down_ref[...] = all_ref[:, :inner]
    up_ref[...] = all_ref[:, inner : 2 * inner]
    nbasis, width = basis_ref.shape
    basis_ref[...] = all_ref[:nbasis, 2 * inner : 2 * inner + width]


def finish(offsets, kept, sent, shared, inner, width, nbasis):
    return pl.pallas_call(
        lambda *refs: finish_kernel(offsets, *refs),
        in_specs=[VMEM] * (2 * len(offsets)),
        out_specs=[VMEM] * 4,
        out_shape=[
            jax.ShapeDtypeStruct((inner, inner), F32),
            jax.ShapeDtypeStruct((width, inner), F32),
            jax.ShapeDtypeStruct((width, inner), F32),
            jax.ShapeDtypeStruct((nbasis, width), F32),
        ],
        scratch_shapes=[
            pltpu.VMEM((width, 2 * inner + 128), F32),
            pltpu.VMEM((2 * shared, 128), F32),
        ],
        compiler_params=limits(),
        name="finish",
    )(*kept, *sent)


def swapped(value, axis, offset):
    return lax.ppermute(value, axis, [(i, i ^ offset) for i in range(lax.axis_size(axis))])


def groups_of(axis, first):
    low, groups = first, []
    while low < lax.axis_size(axis):
        members = min(4, lax.axis_size(axis) // low)
        groups.append((low, members))
        low *= members
    return groups


def total_of(parts):
    return sum(part.astype(F32) for part in parts).astype(BF16)


def scattered_sum(values, axis, low, members, riders):
    digit = (lax.axis_index(axis) // low) % members

    def piece(value, k):
        rows = value.shape[0] // members
        return lax.dynamic_slice_in_dim(value, (digit ^ k) * rows, rows, 0)

    sums = [[piece(value, 0)] for value in values]
    arrived = {}
    for k in range(members - 1, 0, -1):
        sent = [piece(value, k) for value in values] + riders.get(k, [])
        received = swapped(jnp.concatenate(sent, axis=0), axis, k * low)
        start = 0
        for total in sums:
            total.append(received[start : start + total[0].shape[0]])
            start += total[0].shape[0]
        arrived[k] = received[start:]
    return [total_of(total) for total in sums], arrived


def exchanged(value, axis, low, members):
    return {k * low: swapped(value, axis, k * low) for k in range(members - 1, 0, -1)}


def shards(
    embed,
    cotangent,
    basis,
    triplet_row_index,
    triplet_slot_count,
    outgoing_edge_rows,
    residual_weight,
    down_weight,
    up_weight,
    basis_weight,
):
    rows, inner = embed.shape
    trips, nbasis = basis.shape[:2]

    *sends, embed_v, outgoing_v, weight_v = select(embed, outgoing_edge_rows, residual_weight)
    ghosts = pair_exchange(sends)
    basis = basis.reshape(trips * nbasis, rows)
    down_v, index_v, count_v, dres, mine, other, pre, weights = residual(
        embed_v,
        weight_v,
        cotangent,
        basis,
        basis_weight,
        down_weight.T,
        triplet_row_index,
        triplet_slot_count.reshape(1, rows),
    )
    share = total_of([mine, swapped(other, "brick", 1)])

    own, first, second, last, mine, other = triplets(
        pre,
        embed_v,
        down_v,
        ghosts,
        basis,
        index_v,
        count_v,
        up_weight,
        cotangent,
        weights,
    )
    received = swapped(other, "brick", 1)
    shared = mine.shape[0]
    mine = total_of([mine, received[:shared]])
    ring = lax.axis_size("slab")
    riders = {1: [first]}
    if ring == 4:
        riders[3] = [second]
    backs = [None, None, received[shared:], paired(last, "brick", 1)]
    slab_groups = groups_of("slab", 1)
    for low, members in reversed(slab_groups):
        (share, mine), arrived = scattered_sum(
            [share, mine], "slab", low, members, riders if low == 1 else {}
        )
    backs[0] = arrived[1]
    backs[1] = arrived[3] if ring == 4 else paired(second, "slab", 1)
    edge_grad = edge_gradient(own, backs, outgoing_v, pre, weight_v, down_v, dres)

    value = jnp.concatenate([share, mine], axis=0)
    for low, members in groups_of("brick", 2):
        value = total_of([value, *exchanged(value, "brick", low, members).values()])
    value, edge_grad = lax.optimization_barrier((value, edge_grad))
    pieces = {0: value}
    for low, members in slab_groups:
        known = sorted(pieces)
        value = jnp.concatenate([pieces[o] for o in known], axis=0)
        for k, other in exchanged(value, "slab", low, members).items():
            for i, offset in enumerate(known):
                step = pieces[offset].shape[0]
                pieces[offset ^ k] = other[i * step : (i + 1) * step]
    offsets = sorted(pieces)
    kept = [pieces[o] for o in offsets]
    sent = [swapped(piece, "brick", 1) for piece in kept]
    residual_grad, down_grad, up_grad, basis_grad = finish(
        offsets, kept, sent, shared, inner, pre.shape[0], nbasis
    )
    return edge_grad, residual_grad, down_grad.T, up_grad, basis_grad


def solution(mesh):
    both = P(AXES, None)
    in_specs = (both, both, P(None, None, AXES), P(None, AXES), P(AXES), P(None, AXES)) + (P(),) * 4
    out_specs = (both, P(), P(), P(), P())
    return jax.shard_map(shards, mesh=mesh, in_specs=in_specs, out_specs=out_specs, check_vma=False)
```
